256 devices in a mesh: dp: 16 (over z_hi, y), section: 2 (over core), tensor: 8 (over x, z_lo).
Axes of the slice: x: 4, y: 4, z: 8 (z_hi: 4, z_lo: 2; z = z_hi * 2 + z_lo), core: 2. Of those that a mesh axis runs over, the one named last changes fastest.
Arguments:
- residual: bfloat16 [2, 16, 128, 6144], P('section', 'dp'), may hold values from -6 to 6
- queries: bfloat16 [2, 16, 128, 6144], P('section', 'dp', None, 'tensor'), may hold values from -6 to 6
- key_vectors: bfloat16 [2, 16, 128, 6144], P('section', 'dp', None, 'tensor'), may hold values from -6 to 6
- value_vectors: bfloat16 [2, 16, 128, 6144], P('section', 'dp', None, 'tensor'), may hold values from -6 to 6
- block_mask: int32 [2, 16, 4, 4], P('section', 'dp'), may hold values from 0 to 1, as said below
- out_weight: bfloat16 [2, 6144, 6144], P('section', 'tensor', 'dp'), may hold values from -0.078125 to 0.078125
- codebook: bfloat16 [2, 6144, 768], P('section', 'dp'), may hold values from -0.078125 to 0.078125
- norm_gain: float32 [2, 6144], P('section'), may hold values from 0.1 to 1.9
- norm_bias: float32 [2, 6144], P('section'), may hold values from -3 to 3
- receiver_order: int32 [2, 128], P('section', ('dp', 'tensor')), may hold values from 0 to 127, each once within a row
- upstream: bfloat16 [2, 16, 128, 6144], P('section', 'dp'), may hold values from -6 to 6
Outputs:
- received: bfloat16 [2, 128, 16, 768], P('section', ('dp', 'tensor'))
- grad_residual: bfloat16 [2, 16, 128, 6144], P('section', 'dp', 'tensor')
- grad_queries: bfloat16 [2, 16, 128, 6144], P('section', 'dp', None, 'tensor')
- grad_keys: bfloat16 [2, 16, 128, 6144], P('section', 'dp', None, 'tensor')
- grad_values: bfloat16 [2, 16, 128, 6144], P('section', 'dp', None, 'tensor')
The draws below stay inside these ranges and needn't reach their ends.
Inputs may be any that keep to these rules, and one draw needn't show every extreme that they name: `block_mask`: block (i, i) is 1 and block (i, j) with j > i is 0. `receiver_order`: each row is a permutation.
All inputs are finite; a program needn't handle non-finite values.
Results may differ from the reference program's by a relative error of at most 0.015.
Values may be sent and summed in bfloat16 or wider, within the bound.
No kernel may reach another device: no remote copies, remote signals or barrier semaphores. Data moves between devices by JAX's collectives and lax.ppermute only.
A program may use at most 64 MiB of HBM per device.

```python
import jax
import jax.numpy as jnp
from jax import lax

D = 6144
K = 768
HEAD = 128
L = 128
BLK = 32
HEADS = 48
NB = 4
N_DP = 16
N_SECTION = 2
N_TENSOR = 8


def draw_queries(key, part):
    key = jax.random.fold_in(key, 1)
    array_shape = (N_SECTION, N_DP, L, HEADS * HEAD)
    drawn = jnp.clip(jax.random.normal(key, array_shape, jnp.float32), -4.0, 4.0)
    return drawn.astype(jnp.bfloat16)


def draw_key_vectors(key, part):
    key = jax.random.fold_in(key, 2)
    array_shape = (N_SECTION, N_DP, L, HEADS * HEAD)
    drawn = jnp.clip(jax.random.normal(key, array_shape, jnp.float32), -4.0, 4.0)
    return drawn.astype(jnp.bfloat16)


def draw_block_mask(key, part):
    key = jax.random.fold_in(key, 3)
    lower_part = jax.random.randint(key, (N_SECTION, N_DP, NB, NB), 0, 2)
    row_index = jnp.arange(NB, dtype=jnp.int32)[:, None]
    col_index = jnp.arange(NB, dtype=jnp.int32)[None, :]
    result = jnp.where(row_index == col_index, 1, jnp.where(col_index > row_index, 0, lower_part))
    return result.astype(jnp.int32)


def level_of(key, dims, cuts, smallest, largest):
    gain = 1.0
    for axis_at, shards_of in cuts:
        heights = jax.random.uniform(jax.random.fold_in(jax.random.fold_in(key, 6), axis_at), (shards_of,), jnp.float32, smallest / len(cuts), largest / len(cuts))
        gain = gain * jnp.repeat(jnp.exp(heights), dims[axis_at] // shards_of).reshape((-1,) + (1,) * (len(dims) - 1 - axis_at))
    return gain


def normal_values(own_key, dims, scale, bound, cuts=(), kind=jnp.bfloat16):
    array = jax.random.normal(own_key, dims, jnp.float32) * scale
    if len(cuts) > 0:
        array = level_of(own_key, dims, cuts, -0.22, 0.18) * array
    return jnp.clip(array, min=-bound, max=bound).astype(kind)


def setup_inputs(seed: int = 0) -> dict:
    arg_keys = jax.random.split(jax.random.key(seed), 12)
    return {
        "residual": normal_values(arg_keys[0], (N_SECTION, N_DP, L, D), 1.0, 6.0, ((0, 2), (1, 16))),
        "queries": draw_queries(jax.random.fold_in(arg_keys[11], 71), 0),
        "key_vectors": draw_key_vectors(jax.random.fold_in(arg_keys[11], 71), 0),
        "value_vectors": normal_values(arg_keys[3], (N_SECTION, N_DP, L, HEADS * HEAD), 1.0, 6.0, ((0, 2), (1, 16), (3, 8))),
        "block_mask": draw_block_mask(jax.random.fold_in(arg_keys[11], 71), 0),
        "out_weight": normal_values(arg_keys[5], (N_SECTION, HEADS * HEAD, D), (HEADS * HEAD) ** -0.5, 0.078125, ((0, 2), (1, 8), (2, 16))),
        "codebook": normal_values(arg_keys[6], (N_SECTION, D, K), D ** -0.5, 0.078125, ((0, 2), (1, 16))),
        "norm_gain": jnp.clip(1.0 + 0.18 * jax.random.normal(arg_keys[7], (N_SECTION, D), jnp.float32), 0.1, 1.9),
        "norm_bias": normal_values(arg_keys[8], (N_SECTION, D), 0.5, 3.0, ((0, 2),), jnp.float32),
        "receiver_order": jax.vmap(lambda own: jax.random.permutation(own, N_DP * N_TENSOR))(jax.random.split(arg_keys[9], N_SECTION)).reshape((N_SECTION, N_DP * N_TENSOR)).astype(jnp.int32),
        "upstream": normal_values(arg_keys[10], (N_SECTION, N_DP, L, D), 1.0, 6.0, ((0, 2), (1, 16))),
    }


EPSILON = 1e-05

def allowed_pairs(mask_blocks):
    block_table = jnp.repeat(jnp.repeat(mask_blocks, BLK, axis=0), BLK, axis=1) == 1
    position = lax.broadcasted_iota(jnp.int32, (L, L), 0)
    column = lax.broadcasted_iota(jnp.int32, (L, L), 1)
    return block_table & (position >= column)

def attend(query_rows, key_rows, value_rows, allowed):
    length = query_rows.shape[0]
    heads_here = query_rows.shape[1] // HEAD
    query_heads = query_rows.reshape(length, heads_here, HEAD)
    key_heads = key_rows.reshape(length, heads_here, HEAD)
    value_heads = value_rows.reshape(length, heads_here, HEAD)
    scores = jnp.einsum('ihd,jhd->hij', query_heads, key_heads, preferred_element_type=jnp.float32) * HEAD ** (-0.5)
    scores = jnp.where(allowed[None], scores, -1e+30)
    probabilities = jax.nn.softmax(scores, axis=-1).astype(jnp.bfloat16)
    mixture = jnp.einsum('hij,jhd->ihd', probabilities, value_heads, preferred_element_type=jnp.float32)
    return mixture.reshape(length, heads_here * HEAD).astype(jnp.bfloat16)

def times_transposed(left_side, right_side):
    return lax.dot_general(left_side, right_side, (((1,), (1,)), ((), ())), preferred_element_type=jnp.float32)

def layer_norm(hidden, gain_row, bias_row):
    center_mean = lax.optimization_barrier(jnp.mean(hidden, axis=-1, keepdims=True))
    centered = hidden - center_mean
    variance = lax.optimization_barrier(jnp.mean(centered * centered, axis=-1, keepdims=True))
    inv_std = lax.rsqrt(variance + EPSILON)
    normed = centered * inv_std
    return (normed * gain_row + bias_row, normed, inv_std)

def norm_backward(upstream_rows, normed, inv_std, gain_row):
    scaled = upstream_rows * gain_row
    first_mean = lax.optimization_barrier(jnp.mean(scaled, axis=-1, keepdims=True))
    second_mean = lax.optimization_barrier(jnp.mean(scaled * normed, axis=-1, keepdims=True))
    return inv_std * (scaled - first_mean - normed * second_mean)

def reference(residual, queries, key_vectors, value_vectors, block_mask, out_weight, codebook, norm_gain, norm_bias, receiver_order, upstream):
    results = []
    for section_index in range(N_SECTION):
        out_full = out_weight[section_index]
        code_book = codebook[section_index]
        gain_row = norm_gain[section_index]
        bias_row = norm_bias[section_index]
        joined = jnp.dot(out_full, code_book, preferred_element_type=jnp.float32).astype(jnp.bfloat16)

        def one_sequence(sequence_items):
            residual_rows, query_rows, key_rows, value_rows, mask_blocks, upstream_rows = sequence_items
            allowed = allowed_pairs(mask_blocks)
            context = attend(query_rows, key_rows, value_rows, allowed)
            code_sum = jnp.dot(context, joined, preferred_element_type=jnp.float32)
            decoded = times_transposed(code_sum.astype(jnp.bfloat16), code_book)
            hidden = residual_rows.astype(jnp.float32) + decoded
            normed_out, normed, inv_std = layer_norm(hidden, gain_row, bias_row)
            boundary_codes = jnp.dot(normed_out.astype(jnp.bfloat16), code_book, preferred_element_type=jnp.float32).astype(jnp.bfloat16)
            grad_hidden = norm_backward(upstream_rows.astype(jnp.float32), normed, inv_std, gain_row).astype(jnp.bfloat16)
            grad_code = jnp.dot(grad_hidden, code_book, preferred_element_type=jnp.float32).astype(jnp.bfloat16)
            grad_context = times_transposed(grad_code, joined).astype(jnp.bfloat16)

            def attend_only(query_in, key_in, value_in):
                return attend(query_in, key_in, value_in, allowed)
            _, pullback = jax.vjp(attend_only, query_rows, key_rows, value_rows)
            grad_query, grad_key, grad_value = pullback(grad_context)
            return (boundary_codes, grad_hidden, grad_query, grad_key, grad_value)
        results.append(lax.map(one_sequence, (residual[section_index], queries[section_index], key_vectors[section_index], value_vectors[section_index], block_mask[section_index], upstream[section_index])))
    all_codes = jnp.stack([results[0][0], results[1][0]])
    pieces = all_codes.reshape(N_SECTION, N_DP * N_TENSOR, L // N_TENSOR, K)
    received = jnp.stack([pieces[1][receiver_order[0]], pieces[0][receiver_order[1]]])
    grad_residual = jnp.stack([results[0][1], results[1][1]])
    grad_queries = jnp.stack([results[0][2], results[1][2]])
    grad_keys = jnp.stack([results[0][3], results[1][3]])
    grad_values = jnp.stack([results[0][4], results[1][4]])
    return (received, grad_residual, grad_queries, grad_keys, grad_values)
```

```python
import jax
import jax.numpy as jnp
from jax import lax
from jax.sharding import PartitionSpec as P

HEAD = 128
L = 128
BLK = 32


EPSILON = 1e-05


def swapped_2(value, axis, distance):
    return lax.ppermute(value, axis, [(i, i ^ 1 << distance) for i in range(lax.axis_size(axis))])


def exchanged(value, axis):
    return lax.all_to_all(value, axis, 0, 0)


def gathered(value, axis):
    copies = jnp.broadcast_to(value[None], (lax.axis_size(axis),) + value.shape)
    return exchanged(copies, axis)


def summed(pieces):
    return jnp.sum(pieces.astype(jnp.float32), axis=0).astype(jnp.bfloat16)


def allowed_pairs(mask_blocks):
    block_table = jnp.repeat(jnp.repeat(mask_blocks, BLK, axis=0), BLK, axis=1) == 1
    position = lax.broadcasted_iota(jnp.int32, (L, L), 0)
    column = lax.broadcasted_iota(jnp.int32, (L, L), 1)
    return block_table & (position >= column)


def attend(query_rows, key_rows, value_rows, allowed):
    length = query_rows.shape[0]
    heads_here = query_rows.shape[1] // HEAD
    query_heads = query_rows.reshape(length, heads_here, HEAD)
    key_heads = key_rows.reshape(length, heads_here, HEAD)
    value_heads = value_rows.reshape(length, heads_here, HEAD)
    scores = jnp.einsum(
        "ihd,jhd->hij", query_heads, key_heads, preferred_element_type=jnp.float32
    ) * HEAD ** (-0.5)
    scores = jnp.where(allowed[None], scores, -1e30)
    probabilities = jax.nn.softmax(scores, axis=-1).astype(jnp.bfloat16)
    mixture = jnp.einsum(
        "hij,jhd->ihd", probabilities, value_heads, preferred_element_type=jnp.float32
    )
    return mixture.reshape(length, heads_here * HEAD).astype(jnp.bfloat16)


def times_transposed(left_side, right_side):
    return lax.dot_general(
        left_side, right_side, (((1,), (1,)), ((), ())), preferred_element_type=jnp.float32
    )


def on_device(
    residual,
    queries,
    key_vectors,
    value_vectors,
    block_mask,
    out_weight,
    codebook,
    norm_gain,
    norm_bias,
    receiver_order,
    upstream,
):
    n_dp = lax.axis_size("dp")
    n_tensor = lax.axis_size("tensor")
    rank = lax.axis_index("tensor")
    length, width = residual.shape[2:]
    code_book = codebook[0]
    shard, code_width = code_book.shape
    piece = shard // n_tensor
    rows = length // n_tensor
    features = n_dp * piece

    wanted = swapped_2(receiver_order[0], "section", 0)
    wanted_all = lax.all_gather(wanted, "dp", axis=0, tiled=True)
    own_slice = lax.dynamic_slice_in_dim(code_book, rank * piece, piece, 0)
    book_here = lax.all_gather(own_slice, "dp", axis=0, tiled=True)

    joined_part = jnp.dot(out_weight[0], code_book, preferred_element_type=jnp.float32)
    joined_part = joined_part.astype(jnp.bfloat16).reshape(n_dp, -1, code_width)
    joined_rows = summed(exchanged(joined_part, "dp"))
    joined = gathered(joined_rows, "dp").reshape(-1, code_width)

    def own_features(array):
        parts = array.reshape(array.shape[0], n_dp, shard)
        parts = lax.dynamic_slice_in_dim(parts, rank * piece, piece, 2)
        return parts.reshape(array.shape[0], features)

    residual_here = own_features(residual[0, 0]).astype(jnp.float32)
    gain_here = own_features(norm_gain)
    bias_here = own_features(norm_bias)
    scaled = own_features(upstream[0, 0]).astype(jnp.float32) * gain_here

    allowed = allowed_pairs(block_mask[0, 0])
    query_rows = queries[0, 0]
    key_rows = key_vectors[0, 0]
    value_rows = value_vectors[0, 0]

    def attend_only(query_in, key_in, value_in):
        return attend(query_in, key_in, value_in, allowed)

    context, pullback = jax.vjp(attend_only, query_rows, key_rows, value_rows)
    code_part = jnp.dot(context, joined, preferred_element_type=jnp.float32).astype(jnp.bfloat16)
    code_rows = summed(exchanged(code_part.reshape(n_tensor, rows, code_width), "tensor"))
    code_total = gathered(code_rows, "tensor").reshape(length, code_width)

    hidden = residual_here + times_transposed(code_total, book_here)
    near_mean = jnp.mean(hidden, axis=-1)
    near = hidden - near_mean[:, None]
    near_square = jnp.sum(near * near, axis=-1)
    scaled_sum = jnp.sum(scaled, axis=-1)
    scaled_near = jnp.sum(scaled * near, axis=-1)
    own_stats = jnp.stack([near_mean, near_square, scaled_sum, scaled_near])
    all_stats = gathered(own_stats, "tensor")
    means, squares, sums, products = (all_stats[:, i] for i in range(4))
    center_mean = jnp.mean(means, axis=0)
    offsets = means - center_mean
    variance = jnp.sum(squares + features * offsets * offsets, axis=0) / width
    inv_std = lax.rsqrt(variance + EPSILON)
    first_mean = jnp.sum(sums, axis=0) / width
    second_mean = inv_std * jnp.sum(products + offsets * sums, axis=0) / width

    normed = (hidden - center_mean[:, None]) * inv_std[:, None]
    normed_out = (normed * gain_here + bias_here).astype(jnp.bfloat16)
    grad_hidden = inv_std[:, None] * (
        scaled - first_mean[:, None] - normed * second_mean[:, None]
    )
    grad_hidden = grad_hidden.astype(jnp.bfloat16)
    codes_part = jnp.dot(normed_out, book_here, preferred_element_type=jnp.float32)
    grad_part = jnp.dot(grad_hidden, book_here, preferred_element_type=jnp.float32)
    sent = jnp.concatenate(
        [codes_part.astype(jnp.bfloat16), grad_part.astype(jnp.bfloat16), grad_hidden], axis=1
    )
    arrived = exchanged(sent.reshape(n_tensor, rows, -1), "tensor")
    code_rows = summed(arrived[:, :, : 2 * code_width])
    grad_residual = arrived[:, :, 2 * code_width :].reshape(n_tensor, rows, n_dp, piece)
    grad_residual = grad_residual.transpose(1, 2, 0, 3).reshape(rows, width)

    both = gathered(code_rows, "tensor")
    codes = both[:, :, :code_width]
    grad_code = both[:, :, code_width:].reshape(length, code_width)

    slots = jnp.take(codes, wanted_all % n_tensor, axis=0)
    routed = exchanged(slots, "dp")
    chosen = lax.dynamic_index_in_dim(routed, wanted[0] // n_tensor, 0, keepdims=False)
    received = swapped_2(chosen, "section", 0)

    grad_context = times_transposed(grad_code, joined).astype(jnp.bfloat16)
    grad_query, grad_key, grad_value = pullback(grad_context)
    return (
        received[None, None],
        grad_residual[None, None],
        grad_query[None, None],
        grad_key[None, None],
        grad_value[None, None],
    )


def solution(mesh):
    in_specs = (
        P("section", "dp", None, None),
        P("section", "dp", None, "tensor"),
        P("section", "dp", None, "tensor"),
        P("section", "dp", None, "tensor"),
        P("section", "dp", None, None),
        P("section", "tensor", "dp"),
        P("section", "dp", None),
        P("section", None),
        P("section", None),
        P("section", ("dp", "tensor")),
        P("section", "dp", None, None),
    )
    out_specs = (
        P("section", ("dp", "tensor"), None, None),
        P("section", "dp", "tensor", None),
        P("section", "dp", None, "tensor"),
        P("section", "dp", None, "tensor"),
        P("section", "dp", None, "tensor"),
    )
    return jax.shard_map(
        on_device, mesh=mesh, in_specs=in_specs, out_specs=out_specs, check_vma=False
    )
```

```python
import jax
import jax.numpy as jnp
from jax import lax
from jax.experimental import pallas as pl
from jax.experimental.pallas import tpu as pltpu
from jax.sharding import PartitionSpec as P

HEAD = 128
L = 128
BLK = 32


EPSILON = 1e-05
N_HIGH = 4
N_LOW = 4
EXTRA_ROWS = 16
VMEM_BYTES = 40 * 1024 * 1024
HIGH_GROUPS = [[z * N_LOW + y for z in range(N_HIGH)] for y in range(N_LOW)]
LOW_GROUPS = [[z * N_LOW + y for y in range(N_LOW)] for z in range(N_HIGH)]


def swapped_2(value, axis, distance):
    return lax.ppermute(value, axis, [(i, i ^ 1 << distance) for i in range(lax.axis_size(axis))])


def exchanged(value, axis, groups=None):
    return lax.all_to_all(value, axis, 0, 0, axis_index_groups=groups)


def turned(value, high, low):
    pairs = [
        (z * N_LOW + y, (z + high) % N_HIGH * N_LOW + (y + low) % N_LOW)
        for z in range(N_HIGH)
        for y in range(N_LOW)
    ]
    return lax.ppermute(value, "dp", pairs)


def transposed_owner(value, count):
    pairs = [
        ((half * count + d) * count + t, (half * count + t) * count + d)
        for half in range(2)
        for d in range(count)
        for t in range(count)
    ]
    return lax.ppermute(value, ("dp", "tensor"), pairs)


def summed(pieces):
    return jnp.sum(pieces.astype(jnp.float32), axis=0).astype(jnp.bfloat16)


def copies_of(value, count):
    return jnp.broadcast_to(value[None], (count,) + value.shape)


def allowed_pairs(mask_blocks):
    block_table = jnp.repeat(jnp.repeat(mask_blocks, BLK, axis=0), BLK, axis=1) == 1
    position = lax.broadcasted_iota(jnp.int32, (L, L), 0)
    column = lax.broadcasted_iota(jnp.int32, (L, L), 1)
    return block_table & (position >= column)


def times(left_side, right_side):
    return jnp.dot(left_side, right_side, preferred_element_type=jnp.float32)


def times_transposed(left_side, right_side):
    return lax.dot_general(
        left_side, right_side, (((1,), (1,)), ((), ())), preferred_element_type=jnp.float32
    )


def transposed_times(left_side, right_side):
    return lax.dot_general(
        left_side, right_side, (((0,), (0,)), ((), ())), preferred_element_type=jnp.float32
    )


def call(kernel, *shapes, flops=1):
    return pl.pallas_call(
        kernel,
        out_shape=[jax.ShapeDtypeStruct(shape, dtype) for shape, dtype in shapes],
        cost_estimate=pl.CostEstimate(flops=flops, bytes_accessed=4_000_000, transcendentals=0),
        compiler_params=pltpu.CompilerParams(vmem_limit_bytes=VMEM_BYTES),
    )


def placed_call(kernel, count, *shapes):
    return pl.pallas_call(
        kernel,
        out_shape=[jax.ShapeDtypeStruct(shape, dtype) for shape, dtype in shapes],
        in_specs=[pl.BlockSpec(memory_space=pltpu.SMEM)]
        + [pl.BlockSpec(memory_space=pltpu.VMEM)] * (count - 1),
        cost_estimate=pl.CostEstimate(flops=1, bytes_accessed=4_000_000, transcendentals=0),
        compiler_params=pltpu.CompilerParams(vmem_limit_bytes=VMEM_BYTES),
    )


def attend_kernel(query_ref, key_ref, value_ref, allowed_ref, context_ref, chance_ref):
    allowed = allowed_ref[...] > 0.5
    for head in range(query_ref.shape[1] // HEAD):
        columns = slice(head * HEAD, (head + 1) * HEAD)
        scores = times_transposed(query_ref[:, columns], key_ref[:, columns]) * HEAD ** (-0.5)
        scores = jnp.where(allowed, scores, -1e30)
        raised = jnp.exp(scores - jnp.max(scores, axis=-1, keepdims=True))
        chances = raised / jnp.sum(raised, axis=-1, keepdims=True)
        chance_ref[head] = chances
        mixture = times(chances.astype(jnp.bfloat16), value_ref[:, columns])
        context_ref[:, columns] = mixture.astype(jnp.bfloat16)


def code_kernel(context_ref, joined_ref, out_ref):
    code = times(context_ref[...], joined_ref[...]).astype(jnp.bfloat16)
    for copy in range(out_ref.shape[0]):
        out_ref[copy] = code


def feature_kernel(parts_ref, book_ref, residual_ref, gain_ref, scaled_ref, out_ref):
    total = parts_ref[0].astype(jnp.float32)
    for part in range(1, parts_ref.shape[0]):
        total += parts_ref[part].astype(jnp.float32)
    book = book_ref[...]
    width = book.shape[1]
    decoded = times_transposed(total.astype(jnp.bfloat16), book)
    hidden = residual_ref[...] + decoded
    out_ref[:, 3 * width :] = decoded.astype(jnp.bfloat16)
    out_ref[:, :width] = times(hidden.astype(jnp.bfloat16), book).astype(jnp.bfloat16)
    gained = (hidden * gain_ref[...]).astype(jnp.bfloat16)
    out_ref[:, width : 2 * width] = times(gained, book).astype(jnp.bfloat16)
    out_ref[:, 2 * width : 3 * width] = scaled_ref[...]


def row_kernel(arrived_ref, residual_ref, scaled_ref, sums_ref, both_ref, grad_ref):
    count = arrived_ref.shape[0]
    width = sums_ref.shape[1]
    size = residual_ref.shape[1]
    part = size // count // 2
    total = arrived_ref[0, :, : 3 * width].astype(jnp.float32)
    for rank in range(1, count):
        total += arrived_ref[rank, :, : 3 * width].astype(jnp.float32)
    hidden_code = total[:, :width]
    gained_code = total[:, width : 2 * width]
    scaled_code = total[:, 2 * width :]
    decoded = [
        arrived_ref[rank, :, 3 * width + half * part : 3 * width + (half + 1) * part]
        for half in range(2)
        for rank in range(count)
    ]
    hidden = residual_ref[...] + jnp.concatenate(decoded, axis=1).astype(jnp.float32)
    mean = jnp.sum(hidden, axis=-1, keepdims=True) / size
    centered = hidden - mean
    variance = jnp.sum(centered * centered, axis=-1, keepdims=True) / size
    inv_std = lax.rsqrt(variance + EPSILON)
    scaled = scaled_ref[...]
    product = jnp.sum(scaled * centered, axis=-1, keepdims=True) / size
    share = inv_std * inv_std * product
    grad_ref[...] = (inv_std * (scaled - centered * share)).astype(jnp.bfloat16)
    ones_sum, gain_sum, bias_sum = sums_ref[0:1], sums_ref[1:2], sums_ref[2:3]
    codes = inv_std * (gained_code - mean * gain_sum) + bias_sum
    grad_code = inv_std * (scaled_code - share * (hidden_code - mean * ones_sum))
    for copy in range(count):
        both_ref[copy, :, :width] = codes.astype(jnp.bfloat16)
        both_ref[copy, :, width:] = grad_code.astype(jnp.bfloat16)


def slot_kernel(order_ref, both_ref, slots_ref):
    width = slots_ref.shape[2]
    for slot in range(slots_ref.shape[0]):
        slots_ref[slot] = both_ref[order_ref[slot], :, :width]


def back_kernel(
    both_ref,
    joined_ref,
    query_ref,
    key_ref,
    value_ref,
    chance_ref,
    grad_query_ref,
    grad_key_ref,
    grad_value_ref,
):
    length, width = query_ref.shape
    code_width = joined_ref.shape[1]
    grad_code = both_ref[:, :, code_width:].reshape(length, code_width)
    for head in range(width // HEAD):
        columns = slice(head * HEAD, (head + 1) * HEAD)
        grad_context = times_transposed(grad_code, joined_ref[columns]).astype(jnp.bfloat16)
        chances = chance_ref[head]
        grad_value = transposed_times(chances.astype(jnp.bfloat16), grad_context)
        grad_value_ref[:, columns] = grad_value.astype(jnp.bfloat16)
        grad_chances = times_transposed(grad_context, value_ref[:, columns])
        grad_chances = grad_chances.astype(jnp.bfloat16).astype(jnp.float32)
        shift = jnp.sum(grad_chances * chances, axis=-1, keepdims=True)
        grad_scores = chances * (grad_chances - shift) * HEAD ** (-0.5)
        grad_scores = grad_scores.astype(jnp.bfloat16)
        grad_query = times(grad_scores, key_ref[:, columns])
        grad_query_ref[:, columns] = grad_query.astype(jnp.bfloat16)
        grad_key = transposed_times(grad_scores, query_ref[:, columns])
        grad_key_ref[:, columns] = grad_key.astype(jnp.bfloat16)


def extra_kernel(places_ref, book_ref, gain_ref, bias_ref, out_ref):
    shard = book_ref.shape[0]
    columns = pl.ds(pl.multiple_of(places_ref[1] * shard, HEAD), shard)
    row = lax.broadcasted_iota(jnp.int32, (EXTRA_ROWS, shard), 0)
    weights = jnp.where(row == 0, 1.0, jnp.where(row == 1, gain_ref[:, columns], 0.0))
    rest = jnp.where(row == 2, bias_ref[:, columns], weights)
    book = book_ref[...]
    total = jnp.zeros((EXTRA_ROWS, book.shape[1]), jnp.float32)
    for _ in range(3):
        top = rest.astype(jnp.bfloat16)
        rest = rest - top.astype(jnp.float32)
        total += times(top, book)
    high = total.astype(jnp.bfloat16).astype(jnp.float32)
    low = pltpu.roll(total - high, 3, 0)
    row = lax.broadcasted_iota(jnp.int32, total.shape, 0)
    wanted = places_ref[2].astype(jnp.float32)
    both = jnp.where(row < 3, high, jnp.where(row < 6, low, jnp.where(row == 6, wanted, 0.0)))
    out_ref[...] = both.astype(jnp.bfloat16)


def prepare_kernel(
    places_ref,
    residual_ref,
    upstream_ref,
    gain_ref,
    residual_here_ref,
    scaled_here_ref,
    gain_here_ref,
    residual_rows_ref,
    scaled_rows_ref,
):
    length = residual_ref.shape[0]
    rows, width = residual_rows_ref.shape
    part = gain_here_ref.shape[1] // 2
    rank = places_ref[0]
    gain = gain_ref[...]

    def centered(ref, start, scale):
        wide = ref[pl.ds(start, rows), :].astype(jnp.float32)
        wide = wide if scale is None else wide * scale
        return wide - jnp.sum(wide, axis=-1, keepdims=True) / width

    def places(half):
        start = pl.multiple_of((rank + half * (width // part // 2)) * part, HEAD)
        return slice(half * part, (half + 1) * part), pl.ds(start, part)

    for half in range(2):
        here, there = places(half)
        gain_here_ref[:, here] = gain_ref[:, there]
    for start in range(0, length, rows):
        block = slice(start, start + rows)
        wide = residual_ref[block, :].astype(jnp.float32)
        mean = jnp.sum(wide, axis=-1, keepdims=True) / width
        wide = upstream_ref[block, :].astype(jnp.float32) * gain
        scaled_mean = jnp.sum(wide, axis=-1, keepdims=True) / width
        for half in range(2):
            here, there = places(half)
            residual_here_ref[block, here] = residual_ref[block, there].astype(jnp.float32) - mean
            scaled = upstream_ref[block, there].astype(jnp.float32) * gain_ref[:, there]
            scaled_here_ref[block, here] = (scaled - scaled_mean).astype(jnp.bfloat16)
    own = pl.multiple_of(rank * rows, rows)
    residual_rows_ref[...] = centered(residual_ref, own, None)
    scaled_rows_ref[...] = centered(upstream_ref, own, gain)


def assemble_kernel(places_ref, *refs):
    column_refs, (scaled_ref, book_ref, scaled_code_ref, sums_ref, order_ref) = refs[:-5], refs[-5:]
    piece = book_ref.shape[1]
    high, low = places_ref[1] // N_LOW, places_ref[1] % N_LOW
    total = jnp.zeros((EXTRA_ROWS, book_ref.shape[2]), jnp.float32)
    for low_step, column_ref in enumerate(column_refs):
        for high_step in range(N_HIGH):
            place = (high + N_HIGH - high_step) % N_HIGH * N_LOW + (low + N_LOW - low_step) % N_LOW
            book_ref[place] = column_ref[high_step, :piece]
            extra = column_ref[high_step, piece:].astype(jnp.float32)
            order_ref[place] = extra[:, :HEAD]
            total += extra
    sums_ref[...] = total + pltpu.roll(total, EXTRA_ROWS - 3, 0)
    book = book_ref[...].reshape(-1, book_ref.shape[2])
    scaled_code_ref[...] = times(scaled_ref[...], book).astype(jnp.bfloat16)


def on_device(
    residual,
    queries,
    key_vectors,
    value_vectors,
    block_mask,
    out_weight,
    codebook,
    norm_gain,
    norm_bias,
    receiver_order,
    upstream,
):
    n_dp = lax.axis_size("dp")
    n_tensor = lax.axis_size("tensor")
    rank = lax.axis_index("tensor")
    dp_rank = lax.axis_index("dp")
    length, width = residual.shape[2:]
    code_book = codebook[0]
    shard, code_width = code_book.shape
    piece = shard // n_tensor
    rows = length // n_tensor
    features = n_dp * piece
    heads = queries.shape[3] // HEAD
    bf16, f32 = jnp.bfloat16, jnp.float32

    joined_part = times(out_weight[0], code_book).astype(bf16)
    joined_part = joined_part.reshape(N_LOW, -1, code_width)
    joined_rows = summed(exchanged(joined_part, "dp", LOW_GROUPS))

    own_slice = lax.dynamic_slice_in_dim(code_book, rank * piece, piece, 0)
    own_slice = transposed_owner(own_slice, n_tensor)
    wanted = swapped_2(receiver_order[0], "section", 0)
    places = jnp.stack([rank, dp_rank, wanted[0]])
    extra = placed_call(extra_kernel, 4, ((EXTRA_ROWS, code_width), bf16))(
        places, code_book, norm_gain, norm_bias
    )[0]
    payload = jnp.concatenate([own_slice, extra], axis=0)
    column = jnp.stack([payload] + [turned(payload, step, 0) for step in range(1, N_HIGH)])
    residual, upstream, queries, key_vectors, value_vectors, joined_rows = lax.optimization_barrier(
        (residual, upstream, queries, key_vectors, value_vectors, joined_rows)
    )

    joined_rows = joined_rows.reshape(N_HIGH, -1, code_width)
    joined_rows = summed(exchanged(joined_rows, "dp", HIGH_GROUPS))
    joined_rows = exchanged(copies_of(joined_rows, N_HIGH), "dp", HIGH_GROUPS)
    columns = [column] + [turned(column, 0, step) for step in range(1, N_LOW)]
    joined_rows = joined_rows.reshape(-1, code_width)
    joined = exchanged(copies_of(joined_rows, N_LOW), "dp", LOW_GROUPS)
    joined = joined.reshape(-1, code_width)

    allowed = allowed_pairs(block_mask[0, 0]).astype(f32)
    query_rows = queries[0, 0]
    key_rows = key_vectors[0, 0]
    value_rows = value_vectors[0, 0]
    context, chances = call(
        attend_kernel, ((length, heads * HEAD), bf16), ((heads, length, length), f32)
    )(query_rows, key_rows, value_rows, allowed)
    residual_here, scaled_here, gain_here, residual_rows, scaled_rows = placed_call(
        prepare_kernel,
        4,
        ((length, features), f32),
        ((length, features), bf16),
        ((1, features), f32),
        ((rows, width), f32),
        ((rows, width), f32),
    )(places, residual[0, 0], upstream[0, 0], norm_gain)
    book_here, scaled_code, sums, orders = placed_call(
        assemble_kernel,
        N_LOW + 2,
        ((n_dp, piece, code_width), bf16),
        ((length, code_width), bf16),
        ((EXTRA_ROWS, code_width), f32),
        ((n_dp, EXTRA_ROWS, HEAD), f32),
    )(places, *columns, scaled_here)
    book_here = book_here.reshape(features, code_width)
    wanted_all = orders[:, 6, 0].astype(jnp.int32) % n_tensor

    ready = (joined, context, book_here, residual_here, gain_here, scaled_code)
    ready += (residual_rows, scaled_rows, sums, chances, wanted_all)
    ready = lax.optimization_barrier(ready)
    joined, context, book_here, residual_here, gain_here, scaled_code = ready[:6]
    residual_rows, scaled_rows, sums, chances, wanted_all = ready[6:]

    (code_copies,) = call(code_kernel, ((n_tensor, length, code_width), bf16))(context, joined)
    code_parts = exchanged(code_copies, "tensor")
    (sent,) = call(feature_kernel, ((length, 3 * code_width + features), bf16))(
        code_parts, book_here, residual_here, gain_here, scaled_code
    )
    arrived = exchanged(sent.reshape(n_tensor, rows, -1), "tensor")
    both, grad_residual = call(
        row_kernel,
        ((n_tensor, rows, 2 * code_width), bf16),
        ((rows, width), bf16),
    )(arrived, residual_rows, scaled_rows, sums)
    both = exchanged(both, "tensor")

    (slots,) = placed_call(slot_kernel, 2, ((n_dp, rows, code_width), bf16))(wanted_all, both)
    routed = exchanged(slots, "dp")
    grad_query, grad_key, grad_value = call(
        back_kernel, *[((length, heads * HEAD), bf16)] * 3
    )(both, joined, query_rows, key_rows, value_rows, chances)
    routed, grad_query, grad_key, grad_value = lax.optimization_barrier(
        (routed, grad_query, grad_key, grad_value)
    )
    chosen = lax.dynamic_index_in_dim(routed, wanted[0] // n_tensor, 0, keepdims=False)
    received = swapped_2(chosen, "section", 0)
    return (
        received[None, None],
        grad_residual[None, None],
        grad_query[None, None],
        grad_key[None, None],
        grad_value[None, None],
    )


def solution(mesh):
    in_specs = (
        P("section", "dp", None, None),
        P("section", "dp", None, "tensor"),
        P("section", "dp", None, "tensor"),
        P("section", "dp", None, "tensor"),
        P("section", "dp", None, None),
        P("section", "tensor", "dp"),
        P("section", "dp", None),
        P("section", None),
        P("section", None),
        P("section", ("dp", "tensor")),
        P("section", "dp", None, None),
    )
    out_specs = (
        P("section", ("dp", "tensor"), None, None),
        P("section", "dp", "tensor", None),
        P("section", "dp", None, "tensor"),
        P("section", "dp", None, "tensor"),
        P("section", "dp", None, "tensor"),
    )
    return jax.shard_map(
        on_device, mesh=mesh, in_specs=in_specs, out_specs=out_specs, check_vma=False
    )
```

```python
import jax
import jax.numpy as jnp
from jax import lax
from jax.experimental import pallas as pl
from jax.experimental.pallas import tpu as pltpu
from jax.sharding import PartitionSpec as P

HEAD = 128
L = 128
BLK = 32


EPSILON = 1e-05
N_HIGH = 4
N_LOW = 4
N_TENSOR = 8
EXTRA_ROWS = 16
ORDER_ROW = 12
VMEM_BYTES = 20 * 1024 * 1024
HIGH_GROUPS = [[z * N_LOW + y for z in range(N_HIGH)] for y in range(N_LOW)]
LOW_GROUPS = [[z * N_LOW + y for y in range(N_LOW)] for z in range(N_HIGH)]


def swapped_2(value, axis, distance):
    return lax.ppermute(value, axis, [(i, i ^ 1 << distance) for i in range(lax.axis_size(axis))])


def exchanged(value, axis, groups=None):
    return lax.all_to_all(value, axis, 0, 0, axis_index_groups=groups)


def turned(value, high, low):
    pairs = [
        (z * N_LOW + y, (z + high) % N_HIGH * N_LOW + (y + low) % N_LOW)
        for z in range(N_HIGH)
        for y in range(N_LOW)
    ]
    return lax.ppermute(value, "dp", pairs)


def transposed_owner(value, count):
    pairs = [
        ((half * count + d) * count + t, (half * count + t) * count + d)
        for half in range(2)
        for d in range(count)
        for t in range(count)
    ]
    return lax.ppermute(value, ("dp", "tensor"), pairs)


def summed(pieces):
    return jnp.sum(pieces.astype(jnp.float32), axis=0).astype(jnp.bfloat16)


def copies_of(value, count):
    return jnp.broadcast_to(value[None], (count,) + value.shape)


def allowed_pairs(mask_blocks):
    block_table = jnp.repeat(jnp.repeat(mask_blocks, BLK, axis=0), BLK, axis=1) == 1
    position = lax.broadcasted_iota(jnp.int32, (L, L), 0)
    column = lax.broadcasted_iota(jnp.int32, (L, L), 1)
    return block_table & (position >= column)


def times(left_side, right_side):
    return jnp.dot(left_side, right_side, preferred_element_type=jnp.float32)


def times_transposed(left_side, right_side):
    return lax.dot_general(
        left_side, right_side, (((1,), (1,)), ((), ())), preferred_element_type=jnp.float32
    )


def transposed_times(left_side, right_side):
    return lax.dot_general(
        left_side, right_side, (((0,), (0,)), ((), ())), preferred_element_type=jnp.float32
    )


def call(kernel, shapes, *inputs, places=None, after=()):
    skipped = len(after)

    def body(*refs):
        kernel(*refs[skipped:])

    scalars = [] if places is None else [places]
    return pl.pallas_call(
        body,
        out_shape=[jax.ShapeDtypeStruct(shape, dtype) for shape, dtype in shapes],
        in_specs=[pl.BlockSpec(memory_space=pl.ANY)] * skipped
        + [pl.BlockSpec(memory_space=pltpu.SMEM)] * len(scalars)
        + [pl.BlockSpec(memory_space=pltpu.VMEM)] * len(inputs),
        cost_estimate=pl.CostEstimate(flops=1, bytes_accessed=4_000_000, transcendentals=0),
        compiler_params=pltpu.CompilerParams(vmem_limit_bytes=VMEM_BYTES),
    )(*after, *scalars, *inputs)


def attend_kernel(query_ref, key_ref, value_ref, allowed_ref, context_ref, chance_ref):
    allowed = allowed_ref[...] > 0.5
    for head in range(query_ref.shape[1] // HEAD):
        columns = slice(head * HEAD, (head + 1) * HEAD)
        scores = times_transposed(query_ref[:, columns], key_ref[:, columns]) * HEAD ** (-0.5)
        scores = jnp.where(allowed, scores, -1e30)
        raised = jnp.exp(scores - jnp.max(scores, axis=-1, keepdims=True))
        chances = raised / jnp.sum(raised, axis=-1, keepdims=True)
        chance_ref[head] = chances
        mixture = times(chances.astype(jnp.bfloat16), value_ref[:, columns])
        context_ref[:, columns] = mixture.astype(jnp.bfloat16)


def first_kernel(parts_ref, out_ref):
    total = parts_ref[0].astype(jnp.float32)
    for part in range(1, parts_ref.shape[0]):
        total += parts_ref[part].astype(jnp.float32)
    out_ref[...] = total.astype(jnp.bfloat16)


def second_kernel(parts_ref, out_ref):
    total = parts_ref[0].astype(jnp.float32)
    for part in range(1, parts_ref.shape[0]):
        total += parts_ref[part].astype(jnp.float32)
    total = total.astype(jnp.bfloat16)
    for copy in range(out_ref.shape[0]):
        out_ref[copy] = total


def third_kernel(parts_ref, slice_ref, out_ref, slice_copy_ref):
    slice_copy_ref[...] = slice_ref[...]
    for copy in range(out_ref.shape[0]):
        out_ref[copy] = parts_ref[...]


def stack_kernel(places_ref, *refs):
    for step in range(N_HIGH):
        refs[-1][(places_ref[1] + N_HIGH - step) % N_HIGH] = refs[step][...]


def code_kernel(context_ref, joined_ref, column_ref, code_ref, column_copy_ref):
    column_copy_ref[...] = column_ref[...]
    code_ref[...] = times(context_ref[...], joined_ref[...]).astype(jnp.bfloat16)


def total_kernel(parts_ref, out_ref):
    total = parts_ref[0].astype(jnp.float32)
    for part in range(1, parts_ref.shape[0]):
        total += parts_ref[part].astype(jnp.float32)
    total = total.astype(jnp.bfloat16)
    for copy in range(out_ref.shape[0]):
        out_ref[copy] = total


def weight_kernel(places_ref, *refs):
    scaled_ref, gain_ref, bias_ref, book_ref, scaled_code_ref, extra_ref = refs[N_LOW:]
    for high in range(N_HIGH):
        for step in range(N_LOW):
            place = high * N_LOW + (places_ref[2] + N_LOW - step) % N_LOW
            book_ref[place] = refs[step][high]
    features, width = scaled_ref.shape[1], book_ref.shape[2]
    book = book_ref[...].reshape(features, width)
    row = lax.broadcasted_iota(jnp.int32, (EXTRA_ROWS, features), 0)
    rest = jnp.where(row == 0, 1.0, jnp.where(row == 1, gain_ref[...], 0.0))
    rest = jnp.where(row == 2, bias_ref[...], rest)
    total = jnp.zeros((EXTRA_ROWS, width), jnp.float32)
    for _ in range(3):
        top = rest.astype(jnp.bfloat16)
        rest = rest - top.astype(jnp.float32)
        total += times(top, book)
    upper = total.astype(jnp.bfloat16).astype(jnp.float32)
    lower = pltpu.roll(total - upper, 3, 0)
    row = lax.broadcasted_iota(jnp.int32, total.shape, 0)
    both = jnp.where(row < 3, upper, jnp.where(row < 6, lower, 0.0))
    half = width // 2
    extra = both[:, :half] + pltpu.roll(both[:, half:], 6, 0)
    wanted = places_ref[3].astype(jnp.float32)
    extra = jnp.where(row[:, :half] == ORDER_ROW, wanted, extra)
    extra_ref[...] = extra.astype(jnp.bfloat16)
    scaled_code_ref[...] = times(scaled_ref[...], book).astype(jnp.bfloat16)


def feature_kernel(code_ref, book_ref, residual_ref, gain_ref, scaled_ref, extra_ref, out_ref):
    count, rows, _ = out_ref.shape
    features, width = book_ref.shape
    book = book_ref[...]
    code = code_ref[...].reshape(count * rows, width)

    def put(start, value):
        value = value.astype(jnp.bfloat16)
        out_ref[:, :, start : start + value.shape[1]] = value.reshape(count, rows, -1)

    decoded = times_transposed(code, book)
    put(3 * width, decoded)
    hidden = residual_ref[...] + decoded
    put(0, times(hidden.astype(jnp.bfloat16), book))
    put(width, times((hidden * gain_ref[...]).astype(jnp.bfloat16), book))
    put(2 * width, scaled_ref[...])
    for copy in range(count):
        out_ref[copy, :, 3 * width + features :] = extra_ref[...]


def row_kernel(
    arrived_ref, residual_ref, scaled_ref, codes_ref, grad_code_ref, grad_ref, order_ref
):
    count = arrived_ref.shape[0]
    size = residual_ref.shape[1]
    width = codes_ref.shape[2]
    part = size // count // 2
    last = 3 * width + 2 * part
    total = arrived_ref[0, :, : 3 * width].astype(jnp.float32)
    extra = arrived_ref[0, :, last:].astype(jnp.float32)
    order_ref[0] = extra[:, :HEAD]
    for rank in range(1, count):
        total += arrived_ref[rank, :, : 3 * width].astype(jnp.float32)
        part_extra = arrived_ref[rank, :, last:].astype(jnp.float32)
        order_ref[rank] = part_extra[:, :HEAD]
        extra += part_extra
    sums = extra + pltpu.roll(extra, EXTRA_ROWS - 3, 0)
    sums = jnp.concatenate([sums, pltpu.roll(sums, EXTRA_ROWS - 6, 0)], axis=1)
    ones_sum, gain_sum, bias_sum = sums[0:1], sums[1:2], sums[2:3]
    hidden_code = total[:, :width]
    gained_code = total[:, width : 2 * width]
    scaled_code = total[:, 2 * width :]
    decoded = [
        arrived_ref[rank, :, 3 * width + half * part : 3 * width + (half + 1) * part]
        for half in range(2)
        for rank in range(count)
    ]
    hidden = residual_ref[...] + jnp.concatenate(decoded, axis=1).astype(jnp.float32)
    mean = jnp.sum(hidden, axis=-1, keepdims=True) / size
    centered = hidden - mean
    variance = jnp.sum(centered * centered, axis=-1, keepdims=True) / size
    inv_std = lax.rsqrt(variance + EPSILON)
    scaled = scaled_ref[...]
    product = jnp.sum(scaled * centered, axis=-1, keepdims=True) / size
    share = inv_std * inv_std * product
    grad_ref[...] = (inv_std * (scaled - centered * share)).astype(jnp.bfloat16)
    codes = inv_std * (gained_code - mean * gain_sum) + bias_sum
    grad_code = inv_std * (scaled_code - share * (hidden_code - mean * ones_sum))
    grad_code_ref[...] = grad_code.astype(jnp.bfloat16)
    codes = codes.astype(jnp.bfloat16)
    for copy in range(codes_ref.shape[0]):
        codes_ref[copy] = codes


def slot_kernel(order_ref, blocks_ref, grad_code_ref, out_ref):
    width = grad_code_ref.shape[1]
    for slot in range(out_ref.shape[0]):
        out_ref[slot, :, :width] = blocks_ref[order_ref[slot] // N_TENSOR]
        out_ref[slot, :, width:] = grad_code_ref[...]


def chosen_kernel(wanted_ref, both_ref, out_ref):
    out_ref[...] = both_ref[wanted_ref[0] % N_TENSOR, :, : out_ref.shape[1]]


def back_kernel(
    both_ref,
    joined_ref,
    query_ref,
    key_ref,
    value_ref,
    chance_ref,
    grad_query_ref,
    grad_key_ref,
    grad_value_ref,
):
    length, width = query_ref.shape
    code_width = joined_ref.shape[1]
    grad_code = both_ref[:, :, code_width:].reshape(length, code_width)
    for head in range(width // HEAD):
        columns = slice(head * HEAD, (head + 1) * HEAD)
        grad_context = times_transposed(grad_code, joined_ref[columns]).astype(jnp.bfloat16)
        chances = chance_ref[head]
        grad_value = transposed_times(chances.astype(jnp.bfloat16), grad_context)
        grad_value_ref[:, columns] = grad_value.astype(jnp.bfloat16)
        grad_chances = times_transposed(grad_context, value_ref[:, columns])
        grad_chances = grad_chances.astype(jnp.bfloat16).astype(jnp.float32)
        shift = jnp.sum(grad_chances * chances, axis=-1, keepdims=True)
        grad_scores = chances * (grad_chances - shift) * HEAD ** (-0.5)
        grad_scores = grad_scores.astype(jnp.bfloat16)
        grad_query = times(grad_scores, key_ref[:, columns])
        grad_query_ref[:, columns] = grad_query.astype(jnp.bfloat16)
        grad_key = transposed_times(grad_scores, query_ref[:, columns])
        grad_key_ref[:, columns] = grad_key.astype(jnp.bfloat16)


def prepare_kernel(
    places_ref,
    residual_ref,
    upstream_ref,
    gain_ref,
    bias_ref,
    residual_here_ref,
    scaled_here_ref,
    gain_here_ref,
    bias_here_ref,
    residual_rows_ref,
    scaled_rows_ref,
):
    length = residual_ref.shape[0]
    rows, width = residual_rows_ref.shape
    part = gain_here_ref.shape[1] // 2
    rank = places_ref[0]
    gain = gain_ref[...]

    def centered(ref, start, scale):
        wide = ref[pl.ds(start, rows), :].astype(jnp.float32)
        wide = wide if scale is None else wide * scale
        return wide - jnp.sum(wide, axis=-1, keepdims=True) / width

    count = width // part // 2

    def places(half):
        start = pl.multiple_of((rank + half * count) * part, HEAD)
        return slice(half * part, (half + 1) * part), pl.ds(start, part)

    for half in range(2):
        here, there = places(half)
        gain_here_ref[:, here] = gain_ref[:, there]
        bias_here_ref[:, here] = bias_ref[:, there]
    for start in range(0, length, rows):
        block = slice(start, start + rows)
        wide = residual_ref[block, :].astype(jnp.float32)
        mean = jnp.sum(wide, axis=-1, keepdims=True) / width
        wide = upstream_ref[block, :].astype(jnp.float32) * gain
        scaled_mean = jnp.sum(wide, axis=-1, keepdims=True) / width
        for half in range(2):
            here, there = places(half)
            residual_here_ref[block, here] = residual_ref[block, there].astype(jnp.float32) - mean
            scaled = upstream_ref[block, there].astype(jnp.float32) * gain_ref[:, there]
            scaled_here_ref[block, here] = (scaled - scaled_mean).astype(jnp.bfloat16)
    own = pl.multiple_of(rank * rows, rows)
    residual_rows_ref[...] = centered(residual_ref, own, None)
    scaled_rows_ref[...] = centered(upstream_ref, own, gain)


def on_device(
    residual,
    queries,
    key_vectors,
    value_vectors,
    block_mask,
    out_weight,
    codebook,
    norm_gain,
    norm_bias,
    receiver_order,
    upstream,
):
    n_dp = lax.axis_size("dp")
    n_tensor = lax.axis_size("tensor")
    rank = lax.axis_index("tensor")
    length, width = residual.shape[2:]
    code_book = codebook[0]
    shard, code_width = code_book.shape
    piece = shard // n_tensor
    rows = length // n_tensor
    features = n_dp * piece
    heads = queries.shape[3] // HEAD
    share = out_weight.shape[1] // n_dp
    bf16, f32 = jnp.bfloat16, jnp.float32
    dp_rank = lax.axis_index("dp")
    wanted = swapped_2(receiver_order[0], "section", 0)
    places = jnp.stack([rank, dp_rank // N_LOW, dp_rank % N_LOW, wanted[0]])
    allowed = allowed_pairs(block_mask[0, 0]).astype(f32)

    joined_part = times(out_weight[0], code_book).astype(bf16)
    joined_parts = exchanged(joined_part.reshape(N_LOW, -1, code_width), "dp", LOW_GROUPS)
    own_slice = lax.dynamic_slice_in_dim(code_book, rank * piece, piece, 0)
    own_slice = transposed_owner(own_slice, n_tensor)
    residual_here, scaled_here, gain_here, bias_here, residual_rows, scaled_rows = call(
        prepare_kernel,
        [
            ((length, features), f32),
            ((length, features), bf16),
            ((1, features), f32),
            ((1, features), f32),
            ((rows, width), f32),
            ((rows, width), f32),
        ],
        residual[0, 0],
        upstream[0, 0],
        norm_gain,
        norm_bias,
        places=places,
        after=(joined_part,),
    )
    (joined_rows,) = call(
        first_kernel, [((N_HIGH * share, code_width), bf16)], joined_parts, after=(own_slice, gain_here)
    )
    joined_parts = exchanged(joined_rows.reshape(N_HIGH, share, code_width), "dp", HIGH_GROUPS)
    context, chances = call(
        attend_kernel,
        [((length, heads * HEAD), bf16), ((heads, length, length), f32)],
        queries[0, 0],
        key_vectors[0, 0],
        value_vectors[0, 0],
        allowed,
        after=(joined_rows,),
    )
    (joined_rows,) = call(
        second_kernel, [((N_HIGH, share, code_width), bf16)], joined_parts, after=(context,)
    )
    joined_rows = exchanged(joined_rows, "dp", HIGH_GROUPS)
    sent, own_slice = call(
        third_kernel,
        [((N_LOW, N_HIGH * share, code_width), bf16), ((piece, code_width), bf16)],
        joined_rows.reshape(N_HIGH * share, code_width),
        own_slice,
    )
    joined = exchanged(sent, "dp", LOW_GROUPS).reshape(n_dp * share, code_width)

    (column,) = call(
        stack_kernel,
        [((N_HIGH, piece, code_width), bf16)],
        own_slice,
        *[turned(own_slice, step, 0) for step in range(1, N_HIGH)],
        places=places,
    )
    code_part, column = call(
        code_kernel,
        [((length, code_width), bf16), ((N_HIGH, piece, code_width), bf16)],
        context,
        joined,
        column,
    )
    columns = [column] + [turned(column, 0, step) for step in range(1, N_LOW)]
    code_parts = exchanged(code_part.reshape(n_tensor, rows, code_width), "tensor")
    (code_copies,) = call(
        total_kernel, [((n_tensor, rows, code_width), bf16)], code_parts, after=columns[1:]
    )
    code = exchanged(code_copies, "tensor")
    book_here, scaled_code, extra = call(
        weight_kernel,
        [
            ((n_dp, piece, code_width), bf16),
            ((length, code_width), bf16),
            ((EXTRA_ROWS, code_width // 2), bf16),
        ],
        *columns,
        scaled_here,
        gain_here,
        bias_here,
        places=places,
    )
    (sent,) = call(
        feature_kernel,
        [((n_tensor, rows, 3 * code_width + features + code_width // 2), bf16)],
        code,
        book_here.reshape(features, code_width),
        residual_here,
        gain_here,
        scaled_code,
        extra,
    )
    arrived = exchanged(sent, "tensor")
    codes, grad_code, grad_residual, orders = call(
        row_kernel,
        [
            ((n_dp, rows, code_width), bf16),
            ((rows, code_width), bf16),
            ((rows, width), bf16),
            ((n_tensor, EXTRA_ROWS, HEAD), f32),
        ],
        arrived,
        residual_rows,
        scaled_rows,
    )

    blocks = exchanged(codes, "dp")
    order_here = orders[:, ORDER_ROW, 0].astype(jnp.int32)
    (both,) = call(
        slot_kernel,
        [((n_tensor, rows, 2 * code_width), bf16)],
        blocks,
        grad_code,
        places=order_here,
    )
    both = exchanged(both, "tensor")
    (chosen,) = call(chosen_kernel, [((rows, code_width), bf16)], both, places=wanted)
    received = swapped_2(chosen, "section", 0)
    grad_query, grad_key, grad_value = call(
        back_kernel,
        [((length, heads * HEAD), bf16)] * 3,
        both,
        joined,
        queries[0, 0],
        key_vectors[0, 0],
        value_vectors[0, 0],
        chances,
        after=(chosen,),
    )
    return (
        received[None, None],
        grad_residual[None, None],
        grad_query[None, None],
        grad_key[None, None],
        grad_value[None, None],
    )


def solution(mesh):
    in_specs = (
        P("section", "dp", None, None),
        P("section", "dp", None, "tensor"),
        P("section", "dp", None, "tensor"),
        P("section", "dp", None, "tensor"),
        P("section", "dp", None, None),
        P("section", "tensor", "dp"),
        P("section", "dp", None),
        P("section", None),
        P("section", None),
        P("section", ("dp", "tensor")),
        P("section", "dp", None, None),
    )
    out_specs = (
        P("section", ("dp", "tensor"), None, None),
        P("section", "dp", "tensor", None),
        P("section", "dp", None, "tensor"),
        P("section", "dp", None, "tensor"),
        P("section", "dp", None, "tensor"),
    )
    return jax.shard_map(
        on_device, mesh=mesh, in_specs=in_specs, out_specs=out_specs, check_vma=False
    )
```

```python
import jax
import jax.numpy as jnp
from jax import lax
from jax.experimental import pallas as pl
from jax.experimental.pallas import tpu as pltpu
from jax.sharding import PartitionSpec as P

HEAD = 128
L = 128
BLK = 32


EPSILON = 1e-05
N_HIGH = 4
N_LOW = 4
N_TENSOR = 8
EXTRA_ROWS = 16
ORDER_ROW = 12
VMEM_BYTES = 20 * 1024 * 1024
HIGH_GROUPS = [[z * N_LOW + y for z in range(N_HIGH)] for y in range(N_LOW)]
LOW_GROUPS = [[z * N_LOW + y for y in range(N_LOW)] for z in range(N_HIGH)]


def swapped_2(value, axis, distance):
    return lax.ppermute(value, axis, [(i, i ^ 1 << distance) for i in range(lax.axis_size(axis))])


def exchanged(value, axis, groups=None):
    return lax.all_to_all(value, axis, 0, 0, axis_index_groups=groups)


def turned(value, high, low):
    pairs = [
        (z * N_LOW + y, (z + high) % N_HIGH * N_LOW + (y + low) % N_LOW)
        for z in range(N_HIGH)
        for y in range(N_LOW)
    ]
    return lax.ppermute(value, "dp", pairs)


def transposed_owner(value, count):
    pairs = [
        ((half * count + d) * count + t, (half * count + t) * count + d)
        for half in range(2)
        for d in range(count)
        for t in range(count)
    ]
    return lax.ppermute(value, ("dp", "tensor"), pairs)


def summed(pieces):
    return jnp.sum(pieces.astype(jnp.float32), axis=0).astype(jnp.bfloat16)


def copies_of(value, count):
    return jnp.broadcast_to(value[None], (count,) + value.shape)


def allowed_pairs(mask_blocks):
    block_table = jnp.repeat(jnp.repeat(mask_blocks, BLK, axis=0), BLK, axis=1) == 1
    position = lax.broadcasted_iota(jnp.int32, (L, L), 0)
    column = lax.broadcasted_iota(jnp.int32, (L, L), 1)
    return block_table & (position >= column)


def times(left_side, right_side):
    return jnp.dot(left_side, right_side, preferred_element_type=jnp.float32)


def times_transposed(left_side, right_side):
    return lax.dot_general(
        left_side, right_side, (((1,), (1,)), ((), ())), preferred_element_type=jnp.float32
    )


def transposed_times(left_side, right_side):
    return lax.dot_general(
        left_side, right_side, (((0,), (0,)), ((), ())), preferred_element_type=jnp.float32
    )


def call(kernel, shapes, *inputs, places=None, after=(), scratch=()):
    skipped = len(after)

    def body(*refs):
        kernel(*refs[skipped:])

    scalars = [] if places is None else [places]
    return pl.pallas_call(
        body,
        out_shape=[jax.ShapeDtypeStruct(shape, dtype) for shape, dtype in shapes],
        in_specs=[pl.BlockSpec(memory_space=pl.ANY)] * skipped
        + [pl.BlockSpec(memory_space=pltpu.SMEM)] * len(scalars)
        + [pl.BlockSpec(memory_space=pltpu.VMEM)] * len(inputs),
        scratch_shapes=list(scratch),
        cost_estimate=pl.CostEstimate(flops=1, bytes_accessed=4_000_000, transcendentals=0),
        compiler_params=pltpu.CompilerParams(vmem_limit_bytes=VMEM_BYTES),
    )(*after, *scalars, *inputs)


def attend_kernel(query_ref, key_ref, value_ref, allowed_ref, context_ref, chance_ref):
    allowed = allowed_ref[...] > 0.5
    for head in range(query_ref.shape[1] // HEAD):
        columns = slice(head * HEAD, (head + 1) * HEAD)
        scores = times_transposed(query_ref[:, columns], key_ref[:, columns]) * HEAD ** (-0.5)
        scores = jnp.where(allowed, scores, -1e30)
        raised = jnp.exp(scores - jnp.max(scores, axis=-1, keepdims=True))
        chances = raised / jnp.sum(raised, axis=-1, keepdims=True)
        chance_ref[head] = chances
        chance_ref[chance_ref.shape[0] // 2 + head] = chances.T
        mixture = times(chances.astype(jnp.bfloat16), value_ref[:, columns])
        context_ref[:, columns] = mixture.astype(jnp.bfloat16)


def first_kernel(parts_ref, out_ref):
    total = parts_ref[0].astype(jnp.float32)
    for part in range(1, parts_ref.shape[0]):
        total += parts_ref[part].astype(jnp.float32)
    out_ref[...] = total.astype(jnp.bfloat16)


def second_kernel(parts_ref, out_ref):
    total = parts_ref[0].astype(jnp.float32)
    for part in range(1, parts_ref.shape[0]):
        total += parts_ref[part].astype(jnp.float32)
    total = total.astype(jnp.bfloat16)
    for copy in range(out_ref.shape[0]):
        out_ref[copy] = total


def third_kernel(parts_ref, slice_ref, out_ref, slice_copy_ref):
    slice_copy_ref[...] = slice_ref[...]
    for copy in range(out_ref.shape[0]):
        out_ref[copy] = parts_ref[...]


def stack_kernel(places_ref, *refs):
    for step in range(N_HIGH):
        refs[-1][(places_ref[1] + N_HIGH - step) % N_HIGH] = refs[step][...]


def code_kernel(context_ref, joined_ref, column_ref, code_ref, column_copy_ref):
    column_copy_ref[...] = column_ref[...]
    code_ref[...] = times(context_ref[...], joined_ref[...]).astype(jnp.bfloat16)


def total_kernel(parts_ref, out_ref):
    total = parts_ref[0].astype(jnp.float32)
    for part in range(1, parts_ref.shape[0]):
        total += parts_ref[part].astype(jnp.float32)
    total = total.astype(jnp.bfloat16)
    for copy in range(out_ref.shape[0]):
        out_ref[copy] = total


def feature_kernel(places_ref, *refs):
    parts_ref, scaled_ref, residual_ref, gain_ref, bias_ref, out_ref, book_ref = refs[N_LOW:]
    for high in range(N_HIGH):
        for step in range(N_LOW):
            piece = refs[step][high]
            place = high * N_LOW + (places_ref[2] + N_LOW - step) % N_LOW
            start = pl.multiple_of(place * piece.shape[0], EXTRA_ROWS)
            book_ref[pl.ds(start, piece.shape[0])] = piece
    count, rows, _ = out_ref.shape
    features, width = book_ref.shape
    book = book_ref[...]
    code = parts_ref[...].reshape(count * rows, width)

    def put(start, value):
        value = value.astype(jnp.bfloat16)
        out_ref[:, :, start : start + value.shape[1]] = value.reshape(count, rows, -1)

    decoded = times_transposed(code, book)
    put(3 * width, decoded)
    hidden = residual_ref[...] + decoded
    put(0, times(hidden.astype(jnp.bfloat16), book))
    put(width, times((hidden * gain_ref[...]).astype(jnp.bfloat16), book))
    put(2 * width, times(scaled_ref[...], book))
    row = lax.broadcasted_iota(jnp.int32, (EXTRA_ROWS, features), 0)
    rest = jnp.where(row == 0, 1.0, jnp.where(row == 1, gain_ref[...], 0.0))
    rest = jnp.where(row == 2, bias_ref[...], rest)
    total = jnp.zeros((EXTRA_ROWS, width), jnp.float32)
    for _ in range(3):
        top = rest.astype(jnp.bfloat16)
        rest = rest - top.astype(jnp.float32)
        total += times(top, book)
    upper = total.astype(jnp.bfloat16).astype(jnp.float32)
    lower = pltpu.roll(total - upper, 3, 0)
    row = lax.broadcasted_iota(jnp.int32, total.shape, 0)
    both = jnp.where(row < 3, upper, jnp.where(row < 6, lower, 0.0))
    half = width // 2
    extra = both[:, :half] + pltpu.roll(both[:, half:], 6, 0)
    wanted = places_ref[3].astype(jnp.float32)
    extra = jnp.where(row[:, :half] == ORDER_ROW, wanted, extra).astype(jnp.bfloat16)
    for copy in range(count):
        out_ref[copy, :, 3 * width + features :] = extra


def row_kernel(
    arrived_ref, residual_ref, scaled_ref, codes_ref, grad_code_ref, grad_ref, order_ref
):
    count = arrived_ref.shape[0]
    size = residual_ref.shape[1]
    width = codes_ref.shape[2]
    part = size // count // 2
    last = 3 * width + 2 * part
    total = arrived_ref[0, :, : 3 * width].astype(jnp.float32)
    extra = arrived_ref[0, :, last:].astype(jnp.float32)
    order_ref[0] = extra[:, :HEAD]
    for rank in range(1, count):
        total += arrived_ref[rank, :, : 3 * width].astype(jnp.float32)
        part_extra = arrived_ref[rank, :, last:].astype(jnp.float32)
        order_ref[rank] = part_extra[:, :HEAD]
        extra += part_extra
    sums = extra + pltpu.roll(extra, EXTRA_ROWS - 3, 0)
    sums = jnp.concatenate([sums, pltpu.roll(sums, EXTRA_ROWS - 6, 0)], axis=1)
    ones_sum, gain_sum, bias_sum = sums[0:1], sums[1:2], sums[2:3]
    hidden_code = total[:, :width]
    gained_code = total[:, width : 2 * width]
    scaled_code = total[:, 2 * width :]
    decoded = [
        arrived_ref[rank, :, 3 * width + half * part : 3 * width + (half + 1) * part]
        for half in range(2)
        for rank in range(count)
    ]
    hidden = residual_ref[...] + jnp.concatenate(decoded, axis=1).astype(jnp.float32)
    mean = jnp.sum(hidden, axis=-1, keepdims=True) / size
    centered = hidden - mean
    variance = jnp.sum(centered * centered, axis=-1, keepdims=True) / size
    inv_std = lax.rsqrt(variance + EPSILON)
    scaled = scaled_ref[...]
    product = jnp.sum(scaled * centered, axis=-1, keepdims=True) / size
    share = inv_std * inv_std * product
    grad_ref[...] = (inv_std * (scaled - centered * share)).astype(jnp.bfloat16)
    codes = inv_std * (gained_code - mean * gain_sum) + bias_sum
    grad_code = inv_std * (scaled_code - share * (hidden_code - mean * ones_sum))
    grad_code_ref[...] = grad_code.astype(jnp.bfloat16)
    codes = codes.astype(jnp.bfloat16)
    for copy in range(codes_ref.shape[0]):
        codes_ref[copy] = codes


def slot_kernel(order_ref, blocks_ref, grad_code_ref, out_ref):
    width = grad_code_ref.shape[1]
    for slot in range(out_ref.shape[0]):
        wanted = jnp.max(order_ref[slot, ORDER_ROW : ORDER_ROW + 1]).astype(jnp.int32)
        out_ref[slot, :, :width] = blocks_ref[wanted // N_TENSOR]
        out_ref[slot, :, width:] = grad_code_ref[...]


def chosen_kernel(wanted_ref, both_ref, out_ref):
    out_ref[...] = both_ref[wanted_ref[0] % N_TENSOR, :, : out_ref.shape[1]]


def back_kernel(
    both_ref,
    joined_ref,
    query_ref,
    key_ref,
    value_ref,
    chance_ref,
    grad_query_ref,
    grad_key_ref,
    grad_value_ref,
):
    length, width = query_ref.shape
    code_width = joined_ref.shape[1]
    grad_code = both_ref[:, :, code_width:].reshape(length, code_width)
    grad_context = times_transposed(grad_code, joined_ref[...]).astype(jnp.bfloat16)
    heads = [slice(start, start + HEAD) for start in range(0, width, HEAD)]
    grads = [grad_context[:, columns] for columns in heads]
    near = [times_transposed(grad, value_ref[:, columns]) for grad, columns in zip(grads, heads)]
    far = [times_transposed(value_ref[:, columns], grad) for grad, columns in zip(grads, heads)]
    for head, columns in enumerate(heads):
        grad_value = times(chance_ref[len(heads) + head].astype(jnp.bfloat16), grads[head])
        grad_value_ref[:, columns] = grad_value.astype(jnp.bfloat16)

    def scores(grad_chances, chances, axis):
        grad_chances = grad_chances.astype(jnp.bfloat16).astype(jnp.float32)
        shift = jnp.sum(grad_chances * chances, axis=axis, keepdims=True)
        return (chances * (grad_chances - shift) * HEAD ** (-0.5)).astype(jnp.bfloat16)

    near = [scores(grad, chance_ref[head], 1) for head, grad in enumerate(near)]
    far = [scores(grad, chance_ref[len(heads) + head], 0) for head, grad in enumerate(far)]
    for head, columns in enumerate(heads):
        grad_query = times(near[head], key_ref[:, columns])
        grad_query_ref[:, columns] = grad_query.astype(jnp.bfloat16)
        grad_key = times(far[head], query_ref[:, columns])
        grad_key_ref[:, columns] = grad_key.astype(jnp.bfloat16)


def prepare_kernel(
    places_ref,
    residual_ref,
    upstream_ref,
    gain_ref,
    bias_ref,
    residual_here_ref,
    scaled_here_ref,
    gain_here_ref,
    bias_here_ref,
    residual_rows_ref,
    scaled_rows_ref,
):
    length = residual_ref.shape[0]
    rows, width = residual_rows_ref.shape
    part = gain_here_ref.shape[1] // 2
    rank = places_ref[0]
    gain = gain_ref[...]

    def centered(ref, start, scale):
        wide = ref[pl.ds(start, rows), :].astype(jnp.float32)
        wide = wide if scale is None else wide * scale
        return wide - jnp.sum(wide, axis=-1, keepdims=True) / width

    count = width // part // 2

    def places(half):
        start = pl.multiple_of((rank + half * count) * part, HEAD)
        return slice(half * part, (half + 1) * part), pl.ds(start, part)

    for half in range(2):
        here, there = places(half)
        gain_here_ref[:, here] = gain_ref[:, there]
        bias_here_ref[:, here] = bias_ref[:, there]
    for start in range(0, length, rows):
        block = slice(start, start + rows)
        wide = residual_ref[block, :].astype(jnp.float32)
        mean = jnp.sum(wide, axis=-1, keepdims=True) / width
        wide = upstream_ref[block, :].astype(jnp.float32) * gain
        scaled_mean = jnp.sum(wide, axis=-1, keepdims=True) / width
        for half in range(2):
            here, there = places(half)
            residual_here_ref[block, here] = residual_ref[block, there].astype(jnp.float32) - mean
            scaled = upstream_ref[block, there].astype(jnp.float32) * gain_ref[:, there]
            scaled_here_ref[block, here] = (scaled - scaled_mean).astype(jnp.bfloat16)
    own = pl.multiple_of(rank * rows, rows)
    residual_rows_ref[...] = centered(residual_ref, own, None)
    scaled_rows_ref[...] = centered(upstream_ref, own, gain)


def on_device(
    residual,
    queries,
    key_vectors,
    value_vectors,
    block_mask,
    out_weight,
    codebook,
    norm_gain,
    norm_bias,
    receiver_order,
    upstream,
):
    n_dp = lax.axis_size("dp")
    n_tensor = lax.axis_size("tensor")
    rank = lax.axis_index("tensor")
    length, width = residual.shape[2:]
    code_book = codebook[0]
    shard, code_width = code_book.shape
    piece = shard // n_tensor
    rows = length // n_tensor
    features = n_dp * piece
    heads = queries.shape[3] // HEAD
    share = out_weight.shape[1] // n_dp
    bf16, f32 = jnp.bfloat16, jnp.float32
    dp_rank = lax.axis_index("dp")
    wanted = swapped_2(receiver_order[0], "section", 0)
    places = jnp.stack([rank, dp_rank // N_LOW, dp_rank % N_LOW, wanted[0]])
    allowed = allowed_pairs(block_mask[0, 0]).astype(f32)

    joined_part = times(out_weight[0], code_book).astype(bf16)
    joined_parts = exchanged(joined_part.reshape(N_LOW, -1, code_width), "dp", LOW_GROUPS)
    own_slice = lax.dynamic_slice_in_dim(code_book, rank * piece, piece, 0)
    own_slice = transposed_owner(own_slice, n_tensor)
    residual_here, scaled_here, gain_here, bias_here, residual_rows, scaled_rows = call(
        prepare_kernel,
        [
            ((length, features), f32),
            ((length, features), bf16),
            ((1, features), f32),
            ((1, features), f32),
            ((rows, width), f32),
            ((rows, width), f32),
        ],
        residual[0, 0],
        upstream[0, 0],
        norm_gain,
        norm_bias,
        places=places,
        after=(joined_part,),
    )
    (joined_rows,) = call(
        first_kernel, [((N_HIGH * share, code_width), bf16)], joined_parts, after=(own_slice, gain_here)
    )
    joined_parts = exchanged(joined_rows.reshape(N_HIGH, share, code_width), "dp", HIGH_GROUPS)
    context, chances = call(
        attend_kernel,
        [((length, heads * HEAD), bf16), ((2 * heads, length, length), f32)],
        queries[0, 0],
        key_vectors[0, 0],
        value_vectors[0, 0],
        allowed,
        after=(joined_rows,),
    )
    (joined_rows,) = call(
        second_kernel, [((N_HIGH, share, code_width), bf16)], joined_parts, after=(context,)
    )
    joined_rows = exchanged(joined_rows, "dp", HIGH_GROUPS)
    sent, own_slice = call(
        third_kernel,
        [((N_LOW, N_HIGH * share, code_width), bf16), ((piece, code_width), bf16)],
        joined_rows.reshape(N_HIGH * share, code_width),
        own_slice,
    )
    joined = exchanged(sent, "dp", LOW_GROUPS).reshape(n_dp * share, code_width)

    (column,) = call(
        stack_kernel,
        [((N_HIGH, piece, code_width), bf16)],
        own_slice,
        *[turned(own_slice, step, 0) for step in range(1, N_HIGH)],
        places=places,
    )
    code_part, column = call(
        code_kernel,
        [((length, code_width), bf16), ((N_HIGH, piece, code_width), bf16)],
        context,
        joined,
        column,
    )
    columns = [column] + [turned(column, 0, step) for step in range(1, N_LOW)]
    code_parts = exchanged(code_part.reshape(n_tensor, rows, code_width), "tensor")
    (code_copies,) = call(
        total_kernel, [((n_tensor, rows, code_width), bf16)], code_parts, after=columns[1:]
    )
    code = exchanged(code_copies, "tensor")
    (sent,) = call(
        feature_kernel,
        [((n_tensor, rows, 3 * code_width + features + code_width // 2), bf16)],
        *columns,
        code,
        scaled_here,
        residual_here,
        gain_here,
        bias_here,
        places=places,
        scratch=[pltpu.VMEM((features, code_width), bf16)],
    )
    arrived = exchanged(sent, "tensor")
    codes, grad_code, grad_residual, orders = call(
        row_kernel,
        [
            ((n_dp, rows, code_width), bf16),
            ((rows, code_width), bf16),
            ((rows, width), bf16),
            ((n_tensor, EXTRA_ROWS, HEAD), f32),
        ],
        arrived,
        residual_rows,
        scaled_rows,
    )

    blocks = exchanged(codes, "dp")
    (both,) = call(
        slot_kernel,
        [((n_tensor, rows, 2 * code_width), bf16)],
        orders,
        blocks,
        grad_code,
    )
    both = exchanged(both, "tensor")
    (chosen,) = call(chosen_kernel, [((rows, code_width), bf16)], both, places=wanted)
    received = swapped_2(chosen, "section", 0)
    grad_query, grad_key, grad_value = call(
        back_kernel,
        [((length, heads * HEAD), bf16)] * 3,
        both,
        joined,
        queries[0, 0],
        key_vectors[0, 0],
        value_vectors[0, 0],
        chances,
        after=(chosen,),
    )
    return (
        received[None, None],
        grad_residual[None, None],
        grad_query[None, None],
        grad_key[None, None],
        grad_value[None, None],
    )


def solution(mesh):
    in_specs = (
        P("section", "dp", None, None),
        P("section", "dp", None, "tensor"),
        P("section", "dp", None, "tensor"),
        P("section", "dp", None, "tensor"),
        P("section", "dp", None, None),
        P("section", "tensor", "dp"),
        P("section", "dp", None),
        P("section", None),
        P("section", None),
        P("section", ("dp", "tensor")),
        P("section", "dp", None, None),
    )
    out_specs = (
        P("section", ("dp", "tensor"), None, None),
        P("section", "dp", "tensor", None),
        P("section", "dp", None, "tensor"),
        P("section", "dp", None, "tensor"),
        P("section", "dp", None, "tensor"),
    )
    return jax.shard_map(
        on_device, mesh=mesh, in_specs=in_specs, out_specs=out_specs, check_vma=False
    )
```

```python
import jax
import jax.numpy as jnp
from jax import lax
from jax.experimental import pallas as pl
from jax.experimental.pallas import tpu as pltpu
from jax.sharding import PartitionSpec as P

HEAD = 128
L = 128
BLK = 32


EPSILON = 1e-05
N_HIGH = 4
N_LOW = 4
N_TENSOR = 8
EXTRA_ROWS = 16
ORDER_ROW = 12
VMEM_BYTES = 12 * 1024 * 1024
HIGH_GROUPS = [[z * N_LOW + y for z in range(N_HIGH)] for y in range(N_LOW)]
LOW_GROUPS = [[z * N_LOW + y for y in range(N_LOW)] for z in range(N_HIGH)]


def swapped_2(value, axis, distance):
    return lax.ppermute(value, axis, [(i, i ^ 1 << distance) for i in range(lax.axis_size(axis))])


def exchanged(value, axis, groups=None):
    return lax.all_to_all(value, axis, 0, 0, axis_index_groups=groups)


def turned(value, high, low):
    pairs = [
        (z * N_LOW + y, (z + high) % N_HIGH * N_LOW + (y + low) % N_LOW)
        for z in range(N_HIGH)
        for y in range(N_LOW)
    ]
    return lax.ppermute(value, "dp", pairs)


def transposed_owner(value, count):
    pairs = [
        ((half * count + d) * count + t, (half * count + t) * count + d)
        for half in range(2)
        for d in range(count)
        for t in range(count)
    ]
    return lax.ppermute(value, ("dp", "tensor"), pairs)


def summed(pieces):
    return jnp.sum(pieces.astype(jnp.float32), axis=0).astype(jnp.bfloat16)


def copies_of(value, count):
    return jnp.broadcast_to(value[None], (count,) + value.shape)


def allowed_pairs(mask_blocks):
    block_table = jnp.repeat(jnp.repeat(mask_blocks, BLK, axis=0), BLK, axis=1) == 1
    position = lax.broadcasted_iota(jnp.int32, (L, L), 0)
    column = lax.broadcasted_iota(jnp.int32, (L, L), 1)
    return block_table & (position >= column)


def times(left_side, right_side):
    return jnp.dot(left_side, right_side, preferred_element_type=jnp.float32)


def times_transposed(left_side, right_side):
    return lax.dot_general(
        left_side, right_side, (((1,), (1,)), ((), ())), preferred_element_type=jnp.float32
    )


def transposed_times(left_side, right_side):
    return lax.dot_general(
        left_side, right_side, (((0,), (0,)), ((), ())), preferred_element_type=jnp.float32
    )


def call(kernel, shapes, *inputs, places=None, after=(), scratch=()):
    skipped = len(after)

    def body(*refs):
        kernel(*refs[skipped:])

    scalars = [] if places is None else [places]
    return pl.pallas_call(
        body,
        out_shape=[jax.ShapeDtypeStruct(shape, dtype) for shape, dtype in shapes],
        in_specs=[pl.BlockSpec(memory_space=pl.ANY)] * skipped
        + [pl.BlockSpec(memory_space=pltpu.SMEM)] * len(scalars)
        + [pl.BlockSpec(memory_space=pltpu.VMEM)] * len(inputs),
        scratch_shapes=list(scratch),
        cost_estimate=pl.CostEstimate(flops=1, bytes_accessed=4_000_000, transcendentals=0),
        compiler_params=pltpu.CompilerParams(vmem_limit_bytes=VMEM_BYTES),
    )(*after, *scalars, *inputs)


def attend_kernel(query_ref, key_ref, value_ref, allowed_ref, context_ref, chance_ref):
    allowed = allowed_ref[...] > 0.5
    for head in range(query_ref.shape[1] // HEAD):
        columns = slice(head * HEAD, (head + 1) * HEAD)
        scores = times_transposed(query_ref[:, columns], key_ref[:, columns]) * HEAD ** (-0.5)
        scores = jnp.where(allowed, scores, -1e30)
        raised = jnp.exp(scores - jnp.max(scores, axis=-1, keepdims=True))
        chances = raised / jnp.sum(raised, axis=-1, keepdims=True)
        chance_ref[head] = chances
        chance_ref[chance_ref.shape[0] // 2 + head] = chances.T
        mixture = times(chances.astype(jnp.bfloat16), value_ref[:, columns])
        context_ref[:, columns] = mixture.astype(jnp.bfloat16)


def first_kernel(parts_ref, out_ref):
    total = parts_ref[0].astype(jnp.float32)
    for part in range(1, parts_ref.shape[0]):
        total += parts_ref[part].astype(jnp.float32)
    out_ref[...] = total.astype(jnp.bfloat16)


def second_kernel(parts_ref, out_ref):
    total = parts_ref[0].astype(jnp.float32)
    for part in range(1, parts_ref.shape[0]):
        total += parts_ref[part].astype(jnp.float32)
    total = total.astype(jnp.bfloat16)
    for copy in range(out_ref.shape[0]):
        out_ref[copy] = total


def third_kernel(parts_ref, slice_ref, out_ref, slice_copy_ref):
    slice_copy_ref[...] = slice_ref[...]
    for copy in range(out_ref.shape[0]):
        out_ref[copy] = parts_ref[...]


def stack_kernel(places_ref, *refs):
    for step in range(N_HIGH):
        refs[-1][(places_ref[1] + N_HIGH - step) % N_HIGH] = refs[step][...]


def code_kernel(context_ref, joined_ref, column_ref, code_ref, column_copy_ref):
    column_copy_ref[...] = column_ref[...]
    code = times(context_ref[...], joined_ref[...]).astype(jnp.bfloat16)
    for copy in range(code_ref.shape[0]):
        code_ref[copy] = code


def total_kernel(parts_ref, out_ref):
    total = parts_ref[0].astype(jnp.float32)
    for part in range(1, parts_ref.shape[0]):
        total += parts_ref[part].astype(jnp.float32)
    total = total.astype(jnp.bfloat16)
    for copy in range(out_ref.shape[0]):
        out_ref[copy] = total


def pack_kernel(places_ref, *refs):
    here_ref, gain_ref, bias_ref, pack_ref = refs[N_LOW:]
    for high in range(N_HIGH):
        for step in range(N_LOW):
            piece = refs[step][high]
            place = high * N_LOW + (places_ref[2] + N_LOW - step) % N_LOW
            start = pl.multiple_of(place * piece.shape[0], EXTRA_ROWS)
            pack_ref[pl.ds(start, piece.shape[0])] = piece
    _, length, features = here_ref.shape
    width = pack_ref.shape[1]
    book = pack_ref[:features]
    pack_ref[features : features + length] = times(here_ref[0], book).astype(jnp.bfloat16)
    pack_ref[features + length : features + 2 * length] = here_ref[1]
    pack_ref[features + 2 * length : features + 3 * length] = here_ref[2]
    row = lax.broadcasted_iota(jnp.int32, (EXTRA_ROWS, features), 0)
    rest = jnp.where(row == 0, 1.0, jnp.where(row == 1, gain_ref[...], 0.0))
    rest = jnp.where(row == 2, bias_ref[...], rest)
    total = jnp.zeros((EXTRA_ROWS, width), jnp.float32)
    for _ in range(3):
        top = rest.astype(jnp.bfloat16)
        rest = rest - top.astype(jnp.float32)
        total += times(top, book)
    upper = total.astype(jnp.bfloat16).astype(jnp.float32)
    lower = pltpu.roll(total - upper, 3, 0)
    row = lax.broadcasted_iota(jnp.int32, total.shape, 0)
    both = jnp.where(row < 3, upper, jnp.where(row < 6, lower, 0.0))
    half = width // 2
    extra = both[:, :half] + pltpu.roll(both[:, half:], 6, 0)
    wanted = places_ref[3].astype(jnp.float32)
    extra = jnp.where(row[:, :half] == ORDER_ROW, wanted, extra).astype(jnp.bfloat16)
    pack_ref[features + 3 * length :, :half] = extra
    pack_ref[features + 3 * length :, half:] = extra


def feature_kernel(parts_ref, pack_ref, gain_ref, out_ref):
    count, rows, _ = out_ref.shape
    features = gain_ref.shape[1]
    width = pack_ref.shape[1]
    length = count * rows
    book = pack_ref[:features]
    total = parts_ref[0].astype(jnp.float32)
    for part in range(1, count):
        total += parts_ref[part].astype(jnp.float32)
    code = total.astype(jnp.bfloat16)

    def put(start, value):
        value = value.astype(jnp.bfloat16)
        out_ref[:, :, start : start + value.shape[1]] = value.reshape(count, rows, -1)

    decoded = times_transposed(code, book)
    put(3 * width, decoded)
    upper = pack_ref[features + length : features + 2 * length].astype(jnp.float32)
    lower = pack_ref[features + 2 * length : features + 3 * length].astype(jnp.float32)
    hidden = upper + lower + decoded
    put(0, times(hidden.astype(jnp.bfloat16), book))
    put(width, times((hidden * gain_ref[...]).astype(jnp.bfloat16), book))
    put(2 * width, pack_ref[features : features + length])
    extra = pack_ref[features + 3 * length :, : width // 2]
    for copy in range(count):
        out_ref[copy, :, 3 * width + features :] = extra


def row_kernel(
    arrived_ref, residual_ref, scaled_ref, codes_ref, grad_code_ref, grad_ref, order_ref
):
    count = arrived_ref.shape[0]
    size = residual_ref.shape[1]
    width = codes_ref.shape[2]
    part = size // count // 2
    last = 3 * width + 2 * part
    total = arrived_ref[0, :, : 3 * width].astype(jnp.float32)
    extra = arrived_ref[0, :, last:].astype(jnp.float32)
    order_ref[0] = extra[:, :HEAD]
    for rank in range(1, count):
        total += arrived_ref[rank, :, : 3 * width].astype(jnp.float32)
        part_extra = arrived_ref[rank, :, last:].astype(jnp.float32)
        order_ref[rank] = part_extra[:, :HEAD]
        extra += part_extra
    sums = extra + pltpu.roll(extra, EXTRA_ROWS - 3, 0)
    sums = jnp.concatenate([sums, pltpu.roll(sums, EXTRA_ROWS - 6, 0)], axis=1)
    ones_sum, gain_sum, bias_sum = sums[0:1], sums[1:2], sums[2:3]
    hidden_code = total[:, :width]
    gained_code = total[:, width : 2 * width]
    scaled_code = total[:, 2 * width :]
    decoded = [
        arrived_ref[rank, :, 3 * width + half * part : 3 * width + (half + 1) * part]
        for half in range(2)
        for rank in range(count)
    ]
    hidden = residual_ref[...] + jnp.concatenate(decoded, axis=1).astype(jnp.float32)
    mean = jnp.sum(hidden, axis=-1, keepdims=True) / size
    centered = hidden - mean
    variance = jnp.sum(centered * centered, axis=-1, keepdims=True) / size
    inv_std = lax.rsqrt(variance + EPSILON)
    scaled = scaled_ref[...]
    product = jnp.sum(scaled * centered, axis=-1, keepdims=True) / size
    share = inv_std * inv_std * product
    grad_ref[...] = (inv_std * (scaled - centered * share)).astype(jnp.bfloat16)
    codes = inv_std * (gained_code - mean * gain_sum) + bias_sum
    grad_code = inv_std * (scaled_code - share * (hidden_code - mean * ones_sum))
    grad_code_ref[...] = grad_code.astype(jnp.bfloat16)
    codes = codes.astype(jnp.bfloat16)
    for copy in range(codes_ref.shape[0]):
        codes_ref[copy] = codes


def slot_kernel(order_ref, blocks_ref, grad_code_ref, out_ref):
    width = grad_code_ref.shape[1]
    for slot in range(out_ref.shape[0]):
        wanted = jnp.max(order_ref[slot, ORDER_ROW : ORDER_ROW + 1]).astype(jnp.int32)
        out_ref[slot, :, :width] = blocks_ref[wanted // N_TENSOR]
        out_ref[slot, :, width:] = grad_code_ref[...]


def chosen_kernel(wanted_ref, both_ref, out_ref):
    out_ref[...] = both_ref[wanted_ref[0] % N_TENSOR, :, : out_ref.shape[1]]


def back_kernel(
    both_ref,
    joined_ref,
    query_ref,
    key_ref,
    value_ref,
    chance_ref,
    grad_query_ref,
    grad_key_ref,
    grad_value_ref,
):
    length, width = query_ref.shape
    code_width = joined_ref.shape[1]
    grad_code = both_ref[:, :, code_width:].reshape(length, code_width)
    grad_context = times_transposed(grad_code, joined_ref[...]).astype(jnp.bfloat16)
    heads = [slice(start, start + HEAD) for start in range(0, width, HEAD)]
    grads = [grad_context[:, columns] for columns in heads]
    near = [times_transposed(grad, value_ref[:, columns]) for grad, columns in zip(grads, heads)]
    far = [times_transposed(value_ref[:, columns], grad) for grad, columns in zip(grads, heads)]
    for head, columns in enumerate(heads):
        grad_value = times(chance_ref[len(heads) + head].astype(jnp.bfloat16), grads[head])
        grad_value_ref[:, columns] = grad_value.astype(jnp.bfloat16)

    def scores(grad_chances, chances, axis):
        grad_chances = grad_chances.astype(jnp.bfloat16).astype(jnp.float32)
        shift = jnp.sum(grad_chances * chances, axis=axis, keepdims=True)
        return (chances * (grad_chances - shift) * HEAD ** (-0.5)).astype(jnp.bfloat16)

    near = [scores(grad, chance_ref[head], 1) for head, grad in enumerate(near)]
    far = [scores(grad, chance_ref[len(heads) + head], 0) for head, grad in enumerate(far)]
    for head, columns in enumerate(heads):
        grad_query = times(near[head], key_ref[:, columns])
        grad_query_ref[:, columns] = grad_query.astype(jnp.bfloat16)
        grad_key = times(far[head], query_ref[:, columns])
        grad_key_ref[:, columns] = grad_key.astype(jnp.bfloat16)


def prepare_kernel(
    places_ref,
    residual_ref,
    upstream_ref,
    gain_ref,
    bias_ref,
    here_ref,
    gain_here_ref,
    bias_here_ref,
    residual_rows_ref,
    scaled_rows_ref,
):
    length = residual_ref.shape[0]
    rows, width = residual_rows_ref.shape
    part = gain_here_ref.shape[1] // 2
    rank = places_ref[0]
    gain = gain_ref[...]

    def centered(ref, start, scale):
        wide = ref[pl.ds(start, rows), :].astype(jnp.float32)
        wide = wide if scale is None else wide * scale
        return wide - jnp.sum(wide, axis=-1, keepdims=True) / width

    count = width // part // 2

    def places(half):
        start = pl.multiple_of((rank + half * count) * part, HEAD)
        return slice(half * part, (half + 1) * part), pl.ds(start, part)

    for half in range(2):
        here, there = places(half)
        gain_here_ref[:, here] = gain_ref[:, there]
        bias_here_ref[:, here] = bias_ref[:, there]
    for start in range(0, length, rows):
        block = slice(start, start + rows)
        wide = residual_ref[block, :].astype(jnp.float32)
        mean = jnp.sum(wide, axis=-1, keepdims=True) / width
        wide = upstream_ref[block, :].astype(jnp.float32) * gain
        scaled_mean = jnp.sum(wide, axis=-1, keepdims=True) / width
        for half in range(2):
            here, there = places(half)
            scaled = upstream_ref[block, there].astype(jnp.float32) * gain_ref[:, there]
            here_ref[0, block, here] = (scaled - scaled_mean).astype(jnp.bfloat16)
            local = residual_ref[block, there].astype(jnp.float32) - mean
            upper = local.astype(jnp.bfloat16)
            here_ref[1, block, here] = upper
            here_ref[2, block, here] = (local - upper.astype(jnp.float32)).astype(jnp.bfloat16)
    own = pl.multiple_of(rank * rows, rows)
    residual_rows_ref[...] = centered(residual_ref, own, None)
    scaled_rows_ref[...] = centered(upstream_ref, own, gain)


def on_device(
    residual,
    queries,
    key_vectors,
    value_vectors,
    block_mask,
    out_weight,
    codebook,
    norm_gain,
    norm_bias,
    receiver_order,
    upstream,
):
    n_dp = lax.axis_size("dp")
    n_tensor = lax.axis_size("tensor")
    rank = lax.axis_index("tensor")
    length, width = residual.shape[2:]
    code_book = codebook[0]
    shard, code_width = code_book.shape
    piece = shard // n_tensor
    rows = length // n_tensor
    features = n_dp * piece
    heads = queries.shape[3] // HEAD
    share = out_weight.shape[1] // n_dp
    bf16, f32 = jnp.bfloat16, jnp.float32
    dp_rank = lax.axis_index("dp")
    wanted = swapped_2(receiver_order[0], "section", 0)
    places = jnp.stack([rank, dp_rank // N_LOW, dp_rank % N_LOW, wanted[0]])
    allowed = allowed_pairs(block_mask[0, 0]).astype(f32)

    joined_part = times(out_weight[0], code_book).astype(bf16)
    joined_parts = exchanged(joined_part.reshape(N_LOW, -1, code_width), "dp", LOW_GROUPS)
    own_slice = lax.dynamic_slice_in_dim(code_book, rank * piece, piece, 0)
    own_slice = transposed_owner(own_slice, n_tensor)
    here, gain_here, bias_here, residual_rows, scaled_rows = call(
        prepare_kernel,
        [
            ((3, length, features), bf16),
            ((1, features), f32),
            ((1, features), f32),
            ((rows, width), f32),
            ((rows, width), f32),
        ],
        residual[0, 0],
        upstream[0, 0],
        norm_gain,
        norm_bias,
        places=places,
        after=(joined_part,),
    )
    (joined_rows,) = call(
        first_kernel, [((N_HIGH * share, code_width), bf16)], joined_parts, after=(own_slice, gain_here)
    )
    joined_parts = exchanged(joined_rows.reshape(N_HIGH, share, code_width), "dp", HIGH_GROUPS)
    context, chances = call(
        attend_kernel,
        [((length, heads * HEAD), bf16), ((2 * heads, length, length), f32)],
        queries[0, 0],
        key_vectors[0, 0],
        value_vectors[0, 0],
        allowed,
        after=(joined_rows,),
    )
    (joined_rows,) = call(
        second_kernel, [((N_HIGH, share, code_width), bf16)], joined_parts, after=(context,)
    )
    joined_rows = exchanged(joined_rows, "dp", HIGH_GROUPS)
    sent, own_slice = call(
        third_kernel,
        [((N_LOW, N_HIGH * share, code_width), bf16), ((piece, code_width), bf16)],
        joined_rows.reshape(N_HIGH * share, code_width),
        own_slice,
    )
    joined = exchanged(sent, "dp", LOW_GROUPS).reshape(n_dp * share, code_width)

    (column,) = call(
        stack_kernel,
        [((N_HIGH, piece, code_width), bf16)],
        own_slice,
        *[turned(own_slice, step, 0) for step in range(1, N_HIGH)],
        places=places,
    )
    sent, column = call(
        code_kernel,
        [((n_tensor, length, code_width), bf16), ((N_HIGH, piece, code_width), bf16)],
        context,
        joined,
        column,
    )
    columns = [column] + [turned(column, 0, step) for step in range(1, N_LOW)]
    code_parts = exchanged(sent, "tensor")
    (pack,) = call(
        pack_kernel,
        [((features + 3 * length + EXTRA_ROWS, code_width), bf16)],
        *columns,
        here,
        gain_here,
        bias_here,
        places=places,
    )
    (sent,) = call(
        feature_kernel,
        [((n_tensor, rows, 3 * code_width + features + code_width // 2), bf16)],
        code_parts,
        pack,
        gain_here,
    )
    arrived = exchanged(sent, "tensor")
    codes, grad_code, grad_residual, orders = call(
        row_kernel,
        [
            ((n_dp, rows, code_width), bf16),
            ((rows, code_width), bf16),
            ((rows, width), bf16),
            ((n_tensor, EXTRA_ROWS, HEAD), f32),
        ],
        arrived,
        residual_rows,
        scaled_rows,
    )

    blocks = exchanged(codes, "dp")
    (both,) = call(
        slot_kernel,
        [((n_tensor, rows, 2 * code_width), bf16)],
        orders,
        blocks,
        grad_code,
    )
    both = exchanged(both, "tensor")
    (chosen,) = call(chosen_kernel, [((rows, code_width), bf16)], both, places=wanted)
    received = swapped_2(chosen, "section", 0)
    grad_query, grad_key, grad_value = call(
        back_kernel,
        [((length, heads * HEAD), bf16)] * 3,
        both,
        joined,
        queries[0, 0],
        key_vectors[0, 0],
        value_vectors[0, 0],
        chances,
        after=(chosen,),
    )
    return (
        received[None, None],
        grad_residual[None, None],
        grad_query[None, None],
        grad_key[None, None],
        grad_value[None, None],
    )


def solution(mesh):
    in_specs = (
        P("section", "dp", None, None),
        P("section", "dp", None, "tensor"),
        P("section", "dp", None, "tensor"),
        P("section", "dp", None, "tensor"),
        P("section", "dp", None, None),
        P("section", "tensor", "dp"),
        P("section", "dp", None),
        P("section", None),
        P("section", None),
        P("section", ("dp", "tensor")),
        P("section", "dp", None, None),
    )
    out_specs = (
        P("section", ("dp", "tensor"), None, None),
        P("section", "dp", "tensor", None),
        P("section", "dp", None, "tensor"),
        P("section", "dp", None, "tensor"),
        P("section", "dp", None, "tensor"),
    )
    return jax.shard_map(
        on_device, mesh=mesh, in_specs=in_specs, out_specs=out_specs, check_vma=False
    )
```

```python
import jax
import jax.numpy as jnp
from jax import lax
from jax.experimental import pallas as pl
from jax.experimental.pallas import tpu as pltpu
from jax.sharding import PartitionSpec as P

HEAD = 128
L = 128
BLK = 32


EPSILON = 1e-05
N_HIGH = 4
N_LOW = 4
N_TENSOR = 8
EXTRA_ROWS = 16
ORDER_ROW = 12
VMEM_BYTES = 12 * 1024 * 1024
HIGH_GROUPS = [[z * N_LOW + y for z in range(N_HIGH)] for y in range(N_LOW)]
LOW_GROUPS = [[z * N_LOW + y for y in range(N_LOW)] for z in range(N_HIGH)]


def swapped_2(value, axis, distance):
    return lax.ppermute(value, axis, [(i, i ^ 1 << distance) for i in range(lax.axis_size(axis))])


def exchanged(value, axis, groups=None):
    return lax.all_to_all(value, axis, 0, 0, axis_index_groups=groups)


def turned(value, high, low):
    pairs = [
        (z * N_LOW + y, (z + high) % N_HIGH * N_LOW + (y + low) % N_LOW)
        for z in range(N_HIGH)
        for y in range(N_LOW)
    ]
    return lax.ppermute(value, "dp", pairs)


def transposed_owner(value, count):
    pairs = [
        ((half * count + d) * count + t, (half * count + t) * count + d)
        for half in range(2)
        for d in range(count)
        for t in range(count)
    ]
    return lax.ppermute(value, ("dp", "tensor"), pairs)


def summed(pieces):
    return jnp.sum(pieces.astype(jnp.float32), axis=0).astype(jnp.bfloat16)


def copies_of(value, count):
    return jnp.broadcast_to(value[None], (count,) + value.shape)


def allowed_pairs(mask_blocks):
    block_table = jnp.repeat(jnp.repeat(mask_blocks, BLK, axis=0), BLK, axis=1) == 1
    position = lax.broadcasted_iota(jnp.int32, (L, L), 0)
    column = lax.broadcasted_iota(jnp.int32, (L, L), 1)
    return block_table & (position >= column)


def times(left_side, right_side):
    return jnp.dot(left_side, right_side, preferred_element_type=jnp.float32)


def times_transposed(left_side, right_side):
    return lax.dot_general(
        left_side, right_side, (((1,), (1,)), ((), ())), preferred_element_type=jnp.float32
    )


def transposed_times(left_side, right_side):
    return lax.dot_general(
        left_side, right_side, (((0,), (0,)), ((), ())), preferred_element_type=jnp.float32
    )


def call(kernel, shapes, *inputs, places=None, after=(), far=(), far_out=()):
    skipped = len(after)

    def body(*refs):
        kernel(*refs[skipped:])

    scalars = [] if places is None else [places]
    inputs = [
        pltpu.with_memory_space_constraint(array, pltpu.HBM) if place in far else array
        for place, array in enumerate(inputs)
    ]
    return pl.pallas_call(
        body,
        out_shape=[
            pltpu.HBM(shape, dtype) if place in far_out else jax.ShapeDtypeStruct(shape, dtype)
            for place, (shape, dtype) in enumerate(shapes)
        ],
        in_specs=[pl.BlockSpec(memory_space=pl.ANY)] * skipped
        + [pl.BlockSpec(memory_space=pltpu.SMEM)] * len(scalars)
        + [pl.BlockSpec(memory_space=pltpu.VMEM)] * len(inputs),
        out_specs=[pl.BlockSpec(memory_space=pltpu.VMEM)] * len(shapes),
        cost_estimate=pl.CostEstimate(flops=1, bytes_accessed=4_000_000, transcendentals=0),
        compiler_params=pltpu.CompilerParams(vmem_limit_bytes=VMEM_BYTES),
    )(*after, *scalars, *inputs)


def attend_kernel(query_ref, key_ref, value_ref, allowed_ref, context_ref, chance_ref):
    allowed = allowed_ref[...] > 0.5
    for head in range(query_ref.shape[1] // HEAD):
        columns = slice(head * HEAD, (head + 1) * HEAD)
        scores = times_transposed(query_ref[:, columns], key_ref[:, columns]) * HEAD ** (-0.5)
        scores = jnp.where(allowed, scores, -1e30)
        raised = jnp.exp(scores - jnp.max(scores, axis=-1, keepdims=True))
        chances = raised / jnp.sum(raised, axis=-1, keepdims=True)
        chance_ref[head] = chances
        chance_ref[chance_ref.shape[0] // 2 + head] = chances.T
        mixture = times(chances.astype(jnp.bfloat16), value_ref[:, columns])
        context_ref[:, columns] = mixture.astype(jnp.bfloat16)


def first_kernel(parts_ref, out_ref):
    total = parts_ref[0].astype(jnp.float32)
    for part in range(1, parts_ref.shape[0]):
        total += parts_ref[part].astype(jnp.float32)
    out_ref[...] = total.astype(jnp.bfloat16)


def second_kernel(parts_ref, out_ref):
    total = parts_ref[0].astype(jnp.float32)
    for part in range(1, parts_ref.shape[0]):
        total += parts_ref[part].astype(jnp.float32)
    total = total.astype(jnp.bfloat16)
    for copy in range(out_ref.shape[0]):
        out_ref[copy] = total


def third_kernel(parts_ref, slice_ref, out_ref, slice_copy_ref):
    slice_copy_ref[...] = slice_ref[...]
    for copy in range(out_ref.shape[0]):
        out_ref[copy] = parts_ref[...]


def stack_kernel(places_ref, *refs):
    for step in range(N_HIGH):
        refs[-1][(places_ref[1] + N_HIGH - step) % N_HIGH] = refs[step][...]


def code_kernel(context_ref, joined_ref, column_ref, code_ref, column_copy_ref):
    column_copy_ref[...] = column_ref[...]
    code = times(context_ref[...], joined_ref[...]).astype(jnp.bfloat16)
    for copy in range(code_ref.shape[0]):
        code_ref[copy] = code


def total_kernel(parts_ref, out_ref):
    total = parts_ref[0].astype(jnp.float32)
    for part in range(1, parts_ref.shape[0]):
        total += parts_ref[part].astype(jnp.float32)
    total = total.astype(jnp.bfloat16)
    for copy in range(out_ref.shape[0]):
        out_ref[copy] = total


def pack_kernel(places_ref, *refs):
    here_ref, gain_ref, bias_ref, pack_ref = refs[N_LOW:]
    for high in range(N_HIGH):
        for step in range(N_LOW):
            piece = refs[step][high]
            place = high * N_LOW + (places_ref[2] + N_LOW - step) % N_LOW
            start = pl.multiple_of(place * piece.shape[0], EXTRA_ROWS)
            pack_ref[pl.ds(start, piece.shape[0])] = piece
    _, length, features = here_ref.shape
    width = pack_ref.shape[1]
    book = pack_ref[:features]
    pack_ref[features : features + length] = times(here_ref[0], book).astype(jnp.bfloat16)
    pack_ref[features + length : features + 2 * length] = here_ref[1]
    pack_ref[features + 2 * length : features + 3 * length] = here_ref[2]
    row = lax.broadcasted_iota(jnp.int32, (EXTRA_ROWS, features), 0)
    rest = jnp.where(row == 0, 1.0, jnp.where(row == 1, gain_ref[...], 0.0))
    rest = jnp.where(row == 2, bias_ref[...], rest)
    total = jnp.zeros((EXTRA_ROWS, width), jnp.float32)
    for _ in range(3):
        top = rest.astype(jnp.bfloat16)
        rest = rest - top.astype(jnp.float32)
        total += times(top, book)
    upper = total.astype(jnp.bfloat16).astype(jnp.float32)
    lower = pltpu.roll(total - upper, 3, 0)
    row = lax.broadcasted_iota(jnp.int32, total.shape, 0)
    both = jnp.where(row < 3, upper, jnp.where(row < 6, lower, 0.0))
    half = width // 2
    extra = both[:, :half] + pltpu.roll(both[:, half:], 6, 0)
    wanted = places_ref[3].astype(jnp.float32)
    extra = jnp.where(row[:, :half] == ORDER_ROW, wanted, extra).astype(jnp.bfloat16)
    pack_ref[features + 3 * length :, :half] = extra
    pack_ref[features + 3 * length :, half:] = extra


def feature_kernel(parts_ref, pack_ref, gain_ref, out_ref):
    count, rows, _ = out_ref.shape
    features = gain_ref.shape[1]
    width = pack_ref.shape[1]
    length = count * rows
    book = pack_ref[:features]
    total = parts_ref[0].astype(jnp.float32)
    for part in range(1, count):
        total += parts_ref[part].astype(jnp.float32)
    code = total.astype(jnp.bfloat16)

    def put(start, value):
        value = value.astype(jnp.bfloat16)
        out_ref[:, :, start : start + value.shape[1]] = value.reshape(count, rows, -1)

    decoded = times_transposed(code, book)
    put(3 * width, decoded)
    upper = pack_ref[features + length : features + 2 * length].astype(jnp.float32)
    lower = pack_ref[features + 2 * length : features + 3 * length].astype(jnp.float32)
    hidden = upper + lower + decoded
    put(0, times(hidden.astype(jnp.bfloat16), book))
    put(width, times((hidden * gain_ref[...]).astype(jnp.bfloat16), book))
    put(2 * width, pack_ref[features : features + length])
    extra = pack_ref[features + 3 * length :, : width // 2]
    for copy in range(count):
        out_ref[copy, :, 3 * width + features :] = extra


def row_kernel(
    arrived_ref, residual_ref, scaled_ref, codes_ref, grad_code_ref, grad_ref, order_ref
):
    count = arrived_ref.shape[0]
    size = residual_ref.shape[1]
    width = codes_ref.shape[2]
    part = size // count // 2
    last = 3 * width + 2 * part
    total = arrived_ref[0, :, : 3 * width].astype(jnp.float32)
    extra = arrived_ref[0, :, last:].astype(jnp.float32)
    order_ref[0] = extra[:, :HEAD]
    for rank in range(1, count):
        total += arrived_ref[rank, :, : 3 * width].astype(jnp.float32)
        part_extra = arrived_ref[rank, :, last:].astype(jnp.float32)
        order_ref[rank] = part_extra[:, :HEAD]
        extra += part_extra
    sums = extra + pltpu.roll(extra, EXTRA_ROWS - 3, 0)
    sums = jnp.concatenate([sums, pltpu.roll(sums, EXTRA_ROWS - 6, 0)], axis=1)
    ones_sum, gain_sum, bias_sum = sums[0:1], sums[1:2], sums[2:3]
    hidden_code = total[:, :width]
    gained_code = total[:, width : 2 * width]
    scaled_code = total[:, 2 * width :]
    decoded = [
        arrived_ref[rank, :, 3 * width + half * part : 3 * width + (half + 1) * part]
        for half in range(2)
        for rank in range(count)
    ]
    hidden = residual_ref[...] + jnp.concatenate(decoded, axis=1).astype(jnp.float32)
    mean = jnp.sum(hidden, axis=-1, keepdims=True) / size
    centered = hidden - mean
    variance = jnp.sum(centered * centered, axis=-1, keepdims=True) / size
    inv_std = lax.rsqrt(variance + EPSILON)
    scaled = scaled_ref[...]
    product = jnp.sum(scaled * centered, axis=-1, keepdims=True) / size
    share = inv_std * inv_std * product
    grad_ref[...] = (inv_std * (scaled - centered * share)).astype(jnp.bfloat16)
    codes = inv_std * (gained_code - mean * gain_sum) + bias_sum
    grad_code = inv_std * (scaled_code - share * (hidden_code - mean * ones_sum))
    grad_code_ref[...] = grad_code.astype(jnp.bfloat16)
    codes = codes.astype(jnp.bfloat16)
    for copy in range(codes_ref.shape[0]):
        codes_ref[copy] = codes


def slot_kernel(order_ref, blocks_ref, grad_code_ref, out_ref):
    width = grad_code_ref.shape[1]
    for slot in range(out_ref.shape[0]):
        wanted = jnp.max(order_ref[slot, ORDER_ROW : ORDER_ROW + 1]).astype(jnp.int32)
        out_ref[slot, :, :width] = blocks_ref[wanted // N_TENSOR]
        out_ref[slot, :, width:] = grad_code_ref[...]


def chosen_kernel(wanted_ref, both_ref, out_ref):
    out_ref[...] = both_ref[wanted_ref[0] % N_TENSOR, :, : out_ref.shape[1]]


def back_kernel(
    both_ref,
    joined_ref,
    query_ref,
    key_ref,
    value_ref,
    chance_ref,
    grad_query_ref,
    grad_key_ref,
    grad_value_ref,
):
    length, width = query_ref.shape
    code_width = joined_ref.shape[1]
    grad_code = both_ref[:, :, code_width:].reshape(length, code_width)
    grad_context = times_transposed(grad_code, joined_ref[...]).astype(jnp.bfloat16)
    heads = [slice(start, start + HEAD) for start in range(0, width, HEAD)]
    grads = [grad_context[:, columns] for columns in heads]
    near = [times_transposed(grad, value_ref[:, columns]) for grad, columns in zip(grads, heads)]
    far = [times_transposed(value_ref[:, columns], grad) for grad, columns in zip(grads, heads)]
    for head, columns in enumerate(heads):
        grad_value = times(chance_ref[len(heads) + head].astype(jnp.bfloat16), grads[head])
        grad_value_ref[:, columns] = grad_value.astype(jnp.bfloat16)

    def scores(grad_chances, chances, axis):
        grad_chances = grad_chances.astype(jnp.bfloat16).astype(jnp.float32)
        shift = jnp.sum(grad_chances * chances, axis=axis, keepdims=True)
        return (chances * (grad_chances - shift) * HEAD ** (-0.5)).astype(jnp.bfloat16)

    near = [scores(grad, chance_ref[head], 1) for head, grad in enumerate(near)]
    far = [scores(grad, chance_ref[len(heads) + head], 0) for head, grad in enumerate(far)]
    for head, columns in enumerate(heads):
        grad_query = times(near[head], key_ref[:, columns])
        grad_query_ref[:, columns] = grad_query.astype(jnp.bfloat16)
        grad_key = times(far[head], query_ref[:, columns])
        grad_key_ref[:, columns] = grad_key.astype(jnp.bfloat16)


def prepare_kernel(
    places_ref,
    residual_ref,
    upstream_ref,
    gain_ref,
    bias_ref,
    here_ref,
    gain_here_ref,
    bias_here_ref,
    residual_rows_ref,
    scaled_rows_ref,
):
    length = residual_ref.shape[0]
    rows, width = residual_rows_ref.shape
    part = gain_here_ref.shape[1] // 2
    rank = places_ref[0]
    gain = gain_ref[...]

    def centered(ref, start, scale):
        wide = ref[pl.ds(start, rows), :].astype(jnp.float32)
        wide = wide if scale is None else wide * scale
        return wide - jnp.sum(wide, axis=-1, keepdims=True) / width

    count = width // part // 2

    def places(half):
        start = pl.multiple_of((rank + half * count) * part, HEAD)
        return slice(half * part, (half + 1) * part), pl.ds(start, part)

    for half in range(2):
        here, there = places(half)
        gain_here_ref[:, here] = gain_ref[:, there]
        bias_here_ref[:, here] = bias_ref[:, there]
    for start in range(0, length, rows):
        block = slice(start, start + rows)
        wide = residual_ref[block, :].astype(jnp.float32)
        mean = jnp.sum(wide, axis=-1, keepdims=True) / width
        wide = upstream_ref[block, :].astype(jnp.float32) * gain
        scaled_mean = jnp.sum(wide, axis=-1, keepdims=True) / width
        for half in range(2):
            here, there = places(half)
            scaled = upstream_ref[block, there].astype(jnp.float32) * gain_ref[:, there]
            here_ref[0, block, here] = (scaled - scaled_mean).astype(jnp.bfloat16)
            local = residual_ref[block, there].astype(jnp.float32) - mean
            upper = local.astype(jnp.bfloat16)
            here_ref[1, block, here] = upper
            here_ref[2, block, here] = (local - upper.astype(jnp.float32)).astype(jnp.bfloat16)
    own = pl.multiple_of(rank * rows, rows)
    residual_rows_ref[...] = centered(residual_ref, own, None)
    scaled_rows_ref[...] = centered(upstream_ref, own, gain)


def on_device(
    residual,
    queries,
    key_vectors,
    value_vectors,
    block_mask,
    out_weight,
    codebook,
    norm_gain,
    norm_bias,
    receiver_order,
    upstream,
):
    n_dp = lax.axis_size("dp")
    n_tensor = lax.axis_size("tensor")
    rank = lax.axis_index("tensor")
    length, width = residual.shape[2:]
    code_book = codebook[0]
    shard, code_width = code_book.shape
    piece = shard // n_tensor
    rows = length // n_tensor
    features = n_dp * piece
    heads = queries.shape[3] // HEAD
    share = out_weight.shape[1] // n_dp
    bf16, f32 = jnp.bfloat16, jnp.float32
    dp_rank = lax.axis_index("dp")
    wanted = swapped_2(receiver_order[0], "section", 0)
    places = jnp.stack([rank, dp_rank // N_LOW, dp_rank % N_LOW, wanted[0]])
    allowed = allowed_pairs(block_mask[0, 0]).astype(f32)

    joined_part = times(out_weight[0], code_book).astype(bf16)
    joined_parts = exchanged(joined_part.reshape(N_LOW, -1, code_width), "dp", LOW_GROUPS)
    own_slice = lax.dynamic_slice_in_dim(code_book, rank * piece, piece, 0)
    own_slice = transposed_owner(own_slice, n_tensor)
    here, gain_here, bias_here, residual_rows, scaled_rows = call(
        prepare_kernel,
        [
            ((3, length, features), bf16),
            ((1, features), f32),
            ((1, features), f32),
            ((rows, width), f32),
            ((rows, width), f32),
        ],
        residual[0, 0],
        upstream[0, 0],
        norm_gain,
        norm_bias,
        places=places,
        after=(joined_part,),
        far_out=(0, 3, 4),
    )
    (joined_rows,) = call(
        first_kernel, [((N_HIGH * share, code_width), bf16)], joined_parts, after=(own_slice, gain_here)
    )
    joined_parts = exchanged(joined_rows.reshape(N_HIGH, share, code_width), "dp", HIGH_GROUPS)
    context, chances = call(
        attend_kernel,
        [((length, heads * HEAD), bf16), ((2 * heads, length, length), f32)],
        queries[0, 0],
        key_vectors[0, 0],
        value_vectors[0, 0],
        allowed,
        after=(joined_rows,),
    )
    (joined_rows,) = call(
        second_kernel, [((N_HIGH, share, code_width), bf16)], joined_parts, after=(context,)
    )
    joined_rows = exchanged(joined_rows, "dp", HIGH_GROUPS)
    sent, own_slice = call(
        third_kernel,
        [((N_LOW, N_HIGH * share, code_width), bf16), ((piece, code_width), bf16)],
        joined_rows.reshape(N_HIGH * share, code_width),
        own_slice,
    )
    joined = exchanged(sent, "dp", LOW_GROUPS).reshape(n_dp * share, code_width)

    (column,) = call(
        stack_kernel,
        [((N_HIGH, piece, code_width), bf16)],
        own_slice,
        *[turned(own_slice, step, 0) for step in range(1, N_HIGH)],
        places=places,
    )
    sent, column = call(
        code_kernel,
        [((n_tensor, length, code_width), bf16), ((N_HIGH, piece, code_width), bf16)],
        context,
        joined,
        column,
        far_out=(0, 1),
    )
    columns = [column] + [turned(column, 0, step) for step in range(1, N_LOW)]
    code_parts = exchanged(sent, "tensor")
    (pack,) = call(
        pack_kernel,
        [((features + 3 * length + EXTRA_ROWS, code_width), bf16)],
        *columns,
        here,
        gain_here,
        bias_here,
        places=places,
        far=(0, N_LOW),
        far_out=(0,),
    )
    (sent,) = call(
        feature_kernel,
        [((n_tensor, rows, 3 * code_width + features + code_width // 2), bf16)],
        code_parts,
        pack,
        gain_here,
        far=(1,),
    )
    arrived = exchanged(sent, "tensor")
    codes, grad_code, grad_residual, orders = call(
        row_kernel,
        [
            ((n_dp, rows, code_width), bf16),
            ((rows, code_width), bf16),
            ((rows, width), bf16),
            ((n_tensor, EXTRA_ROWS, HEAD), f32),
        ],
        arrived,
        residual_rows,
        scaled_rows,
    )

    blocks = exchanged(codes, "dp")
    (both,) = call(
        slot_kernel,
        [((n_tensor, rows, 2 * code_width), bf16)],
        orders,
        blocks,
        grad_code,
    )
    both = exchanged(both, "tensor")
    (chosen,) = call(chosen_kernel, [((rows, code_width), bf16)], both, places=wanted)
    received = swapped_2(chosen, "section", 0)
    grad_query, grad_key, grad_value = call(
        back_kernel,
        [((length, heads * HEAD), bf16)] * 3,
        both,
        joined,
        queries[0, 0],
        key_vectors[0, 0],
        value_vectors[0, 0],
        chances,
        after=(chosen,),
    )
    return (
        received[None, None],
        grad_residual[None, None],
        grad_query[None, None],
        grad_key[None, None],
        grad_value[None, None],
    )


def solution(mesh):
    in_specs = (
        P("section", "dp", None, None),
        P("section", "dp", None, "tensor"),
        P("section", "dp", None, "tensor"),
        P("section", "dp", None, "tensor"),
        P("section", "dp", None, None),
        P("section", "tensor", "dp"),
        P("section", "dp", None),
        P("section", None),
        P("section", None),
        P("section", ("dp", "tensor")),
        P("section", "dp", None, None),
    )
    out_specs = (
        P("section", ("dp", "tensor"), None, None),
        P("section", "dp", "tensor", None),
        P("section", "dp", None, "tensor"),
        P("section", "dp", None, "tensor"),
        P("section", "dp", None, "tensor"),
    )
    return jax.shard_map(
        on_device, mesh=mesh, in_specs=in_specs, out_specs=out_specs, check_vma=False
    )
```

```python
import jax
import jax.numpy as jnp
from jax import lax
from jax.experimental import pallas as pl
from jax.experimental.pallas import tpu as pltpu
from jax.sharding import PartitionSpec as P

HEAD = 128
L = 128
BLK = 32


EPSILON = 1e-05
N_HIGH = 4
N_LOW = 4
N_TENSOR = 8
EXTRA_ROWS = 16
ORDER_ROW = 12
VMEM_BYTES = 12 * 1024 * 1024
HIGH_GROUPS = [[z * N_LOW + y for z in range(N_HIGH)] for y in range(N_LOW)]
LOW_GROUPS = [[z * N_LOW + y for y in range(N_LOW)] for z in range(N_HIGH)]


def swapped_2(value, axis, distance):
    return lax.ppermute(value, axis, [(i, i ^ 1 << distance) for i in range(lax.axis_size(axis))])


def exchanged(value, axis, groups=None):
    return lax.all_to_all(value, axis, 0, 0, axis_index_groups=groups)


def turned(value, high, low):
    pairs = [
        (z * N_LOW + y, (z + high) % N_HIGH * N_LOW + (y + low) % N_LOW)
        for z in range(N_HIGH)
        for y in range(N_LOW)
    ]
    return lax.ppermute(value, "dp", pairs)


def slice_at(place, rank):
    count = N_TENSOR
    owner = place // count * count + rank
    near = [(ring(owner // N_LOW, e // N_LOW) * 2 + ring(owner, e), e) for e in octet_of(place)]
    far = [(-ring(p // 2, rank // 2) - abs(p % 2 - rank % 2), p) for p in range(count)]
    pairs = {e: p for (_, e), (_, p) in zip(sorted(near), sorted(far))}
    return pairs[place]


def octet_of(place):
    start = place // N_TENSOR * N_TENSOR
    return range(start, start + N_TENSOR)


def ring(one, other):
    away = (one - other) % N_LOW
    return min(away, N_LOW - away)


def transposed_owner(value, count):
    pairs = []
    for place in range(2 * count):
        for rank in range(count):
            owner = place // count * count + rank
            pairs.append((owner * count + slice_at(place, rank), place * count + rank))
    return lax.ppermute(value, ("dp", "tensor"), pairs)


def summed(pieces):
    return jnp.sum(pieces.astype(jnp.float32), axis=0).astype(jnp.bfloat16)


def copies_of(value, count):
    return jnp.broadcast_to(value[None], (count,) + value.shape)


def allowed_pairs(mask_blocks):
    block_table = jnp.repeat(jnp.repeat(mask_blocks, BLK, axis=0), BLK, axis=1) == 1
    position = lax.broadcasted_iota(jnp.int32, (L, L), 0)
    column = lax.broadcasted_iota(jnp.int32, (L, L), 1)
    return block_table & (position >= column)


def times(left_side, right_side):
    return jnp.dot(left_side, right_side, preferred_element_type=jnp.float32)


def times_transposed(left_side, right_side):
    return lax.dot_general(
        left_side, right_side, (((1,), (1,)), ((), ())), preferred_element_type=jnp.float32
    )


def transposed_times(left_side, right_side):
    return lax.dot_general(
        left_side, right_side, (((0,), (0,)), ((), ())), preferred_element_type=jnp.float32
    )


def call(
    kernel, shapes, *inputs, places=None, after=(), far=(), far_out=(), raw=(), scratch=()
):
    skipped = len(after)

    def body(*refs):
        kernel(*refs[skipped:])

    scalars = [] if places is None else [places]
    inputs = [
        pltpu.with_memory_space_constraint(array, pltpu.HBM) if place in far else array
        for place, array in enumerate(inputs)
    ]
    return pl.pallas_call(
        body,
        out_shape=[
            pltpu.HBM(shape, dtype) if place in far_out else jax.ShapeDtypeStruct(shape, dtype)
            for place, (shape, dtype) in enumerate(shapes)
        ],
        in_specs=[pl.BlockSpec(memory_space=pl.ANY)] * skipped
        + [pl.BlockSpec(memory_space=pltpu.SMEM)] * len(scalars)
        + [
            pl.BlockSpec(memory_space=pl.ANY if place in raw else pltpu.VMEM)
            for place in range(len(inputs))
        ],
        out_specs=[
            pl.BlockSpec(memory_space=pl.ANY if raw and place in far_out else pltpu.VMEM)
            for place in range(len(shapes))
        ],
        scratch_shapes=list(scratch),
        cost_estimate=pl.CostEstimate(flops=1, bytes_accessed=4_000_000, transcendentals=0),
        compiler_params=pltpu.CompilerParams(vmem_limit_bytes=VMEM_BYTES),
    )(*after, *scalars, *inputs)


def attend_kernel(query_ref, key_ref, value_ref, allowed_ref, context_ref, chance_ref):
    allowed = allowed_ref[...] > 0.5
    for head in range(query_ref.shape[1] // HEAD):
        columns = slice(head * HEAD, (head + 1) * HEAD)
        scores = times_transposed(query_ref[:, columns], key_ref[:, columns]) * HEAD ** (-0.5)
        scores = jnp.where(allowed, scores, -1e30)
        raised = jnp.exp(scores - jnp.max(scores, axis=-1, keepdims=True))
        chances = raised / jnp.sum(raised, axis=-1, keepdims=True)
        chance_ref[head] = chances
        chance_ref[chance_ref.shape[0] // 2 + head] = chances.T
        mixture = times(chances.astype(jnp.bfloat16), value_ref[:, columns])
        context_ref[:, columns] = mixture.astype(jnp.bfloat16)


def first_kernel(parts_ref, out_ref):
    total = parts_ref[0].astype(jnp.float32)
    for part in range(1, parts_ref.shape[0]):
        total += parts_ref[part].astype(jnp.float32)
    out_ref[...] = total.astype(jnp.bfloat16)


def second_kernel(parts_ref, out_ref):
    total = parts_ref[0].astype(jnp.float32)
    for part in range(1, parts_ref.shape[0]):
        total += parts_ref[part].astype(jnp.float32)
    total = total.astype(jnp.bfloat16)
    for copy in range(out_ref.shape[0]):
        out_ref[copy] = total


def third_kernel(parts_ref, slice_ref, out_ref, slice_copy_ref):
    slice_copy_ref[...] = slice_ref[...]
    for copy in range(out_ref.shape[0]):
        out_ref[copy] = parts_ref[...]


def stack_kernel(places_ref, *refs):
    for step in range(N_HIGH):
        refs[-1][(places_ref[1] + N_HIGH - step) % N_HIGH] = refs[step][...]


def code_kernel(context_ref, joined_ref, column_ref, code_ref, column_copy_ref):
    column_copy_ref[...] = column_ref[...]
    code = times(context_ref[...], joined_ref[...]).astype(jnp.bfloat16)
    for copy in range(code_ref.shape[0]):
        code_ref[copy] = code


def total_kernel(parts_ref, out_ref):
    total = parts_ref[0].astype(jnp.float32)
    for part in range(1, parts_ref.shape[0]):
        total += parts_ref[part].astype(jnp.float32)
    total = total.astype(jnp.bfloat16)
    for copy in range(out_ref.shape[0]):
        out_ref[copy] = total


def pack_kernel(places_ref, *refs):
    here_ref, gain_ref, bias_ref, pack_ref = refs[N_LOW:]
    for high in range(N_HIGH):
        for step in range(N_LOW):
            piece = refs[step][high]
            place = high * N_LOW + (places_ref[2] + N_LOW - step) % N_LOW
            part = place // N_TENSOR * N_TENSOR + places_ref[4 + place]
            start = pl.multiple_of(part * piece.shape[0], EXTRA_ROWS)
            pack_ref[pl.ds(start, piece.shape[0])] = piece
    _, length, features = here_ref.shape
    width = pack_ref.shape[1]
    book = pack_ref[:features]
    pack_ref[features : features + length] = times(here_ref[0], book).astype(jnp.bfloat16)
    pack_ref[features + length : features + 2 * length] = here_ref[1]
    pack_ref[features + 2 * length : features + 3 * length] = here_ref[2]
    row = lax.broadcasted_iota(jnp.int32, (EXTRA_ROWS, features), 0)
    rest = jnp.where(row == 0, 1.0, jnp.where(row == 1, gain_ref[...], 0.0))
    rest = jnp.where(row == 2, bias_ref[...], rest)
    total = jnp.zeros((EXTRA_ROWS, width), jnp.float32)
    for _ in range(3):
        top = rest.astype(jnp.bfloat16)
        rest = rest - top.astype(jnp.float32)
        total += times(top, book)
    upper = total.astype(jnp.bfloat16).astype(jnp.float32)
    lower = pltpu.roll(total - upper, 3, 0)
    row = lax.broadcasted_iota(jnp.int32, total.shape, 0)
    both = jnp.where(row < 3, upper, jnp.where(row < 6, lower, 0.0))
    half = width // 2
    extra = both[:, :half] + pltpu.roll(both[:, half:], 6, 0)
    wanted = places_ref[3].astype(jnp.float32)
    extra = jnp.where(row[:, :half] == ORDER_ROW, wanted, extra).astype(jnp.bfloat16)
    pack_ref[features + 3 * length :, :half] = extra
    pack_ref[features + 3 * length :, half:] = extra


def feature_kernel(parts_ref, pack_hbm, gain_ref, out_ref, pack_ref, semaphores):
    count, rows, _ = out_ref.shape
    features = gain_ref.shape[1]
    width = pack_ref.shape[1]
    length = count * rows
    rest = pl.ds(features, pack_ref.shape[0] - features)
    copies = [
        pltpu.make_async_copy(pack_hbm.at[there], pack_ref.at[there], semaphores.at[place])
        for place, there in enumerate((pl.ds(0, features), rest))
    ]
    for copy in copies:
        copy.start()
    total = parts_ref[0].astype(jnp.float32)
    for part in range(1, count):
        total += parts_ref[part].astype(jnp.float32)
    code = total.astype(jnp.bfloat16)
    copies[0].wait()
    book = pack_ref[:features]

    def put(start, value):
        value = value.astype(jnp.bfloat16)
        out_ref[:, :, start : start + value.shape[1]] = value.reshape(count, rows, -1)

    decoded = times_transposed(code, book)
    put(3 * width, decoded)
    copies[1].wait()
    upper = pack_ref[features + length : features + 2 * length].astype(jnp.float32)
    lower = pack_ref[features + 2 * length : features + 3 * length].astype(jnp.float32)
    hidden = upper + lower + decoded
    put(0, times(hidden.astype(jnp.bfloat16), book))
    put(width, times((hidden * gain_ref[...]).astype(jnp.bfloat16), book))
    put(2 * width, pack_ref[features : features + length])
    extra = pack_ref[features + 3 * length :, : width // 2]
    for copy in range(count):
        out_ref[copy, :, 3 * width + features :] = extra


def row_kernel(
    arrived_ref, residual_ref, scaled_ref, codes_ref, grad_code_ref, grad_ref, order_ref
):
    count = arrived_ref.shape[0]
    size = residual_ref.shape[1]
    width = codes_ref.shape[2]
    part = size // count // 2
    last = 3 * width + 2 * part
    total = arrived_ref[0, :, : 3 * width].astype(jnp.float32)
    extra = arrived_ref[0, :, last:].astype(jnp.float32)
    order_ref[0] = extra[:, :HEAD]
    for rank in range(1, count):
        total += arrived_ref[rank, :, : 3 * width].astype(jnp.float32)
        part_extra = arrived_ref[rank, :, last:].astype(jnp.float32)
        order_ref[rank] = part_extra[:, :HEAD]
        extra += part_extra
    sums = extra + pltpu.roll(extra, EXTRA_ROWS - 3, 0)
    sums = jnp.concatenate([sums, pltpu.roll(sums, EXTRA_ROWS - 6, 0)], axis=1)
    ones_sum, gain_sum, bias_sum = sums[0:1], sums[1:2], sums[2:3]
    hidden_code = total[:, :width]
    gained_code = total[:, width : 2 * width]
    scaled_code = total[:, 2 * width :]
    decoded = [
        arrived_ref[rank, :, 3 * width + half * part : 3 * width + (half + 1) * part]
        for half in range(2)
        for rank in range(count)
    ]
    hidden = residual_ref[...] + jnp.concatenate(decoded, axis=1).astype(jnp.float32)
    mean = jnp.sum(hidden, axis=-1, keepdims=True) / size
    centered = hidden - mean
    variance = jnp.sum(centered * centered, axis=-1, keepdims=True) / size
    inv_std = lax.rsqrt(variance + EPSILON)
    scaled = scaled_ref[...]
    product = jnp.sum(scaled * centered, axis=-1, keepdims=True) / size
    share = inv_std * inv_std * product
    grad_ref[...] = (inv_std * (scaled - centered * share)).astype(jnp.bfloat16)
    codes = inv_std * (gained_code - mean * gain_sum) + bias_sum
    grad_code = inv_std * (scaled_code - share * (hidden_code - mean * ones_sum))
    grad_code_ref[...] = grad_code.astype(jnp.bfloat16)
    codes = codes.astype(jnp.bfloat16)
    for copy in range(codes_ref.shape[0]):
        codes_ref[copy] = codes


def slot_kernel(order_ref, blocks_ref, grad_code_ref, out_ref):
    width = grad_code_ref.shape[1]
    for slot in range(out_ref.shape[0]):
        wanted = jnp.max(order_ref[slot, ORDER_ROW : ORDER_ROW + 1]).astype(jnp.int32)
        out_ref[slot, :, :width] = blocks_ref[wanted // N_TENSOR]
        out_ref[slot, :, width:] = grad_code_ref[...]


def chosen_kernel(wanted_ref, both_ref, out_ref):
    out_ref[...] = both_ref[wanted_ref[0] % N_TENSOR, :, : out_ref.shape[1]]


def back_kernel(
    both_ref,
    joined_ref,
    query_ref,
    key_ref,
    value_ref,
    chance_ref,
    grad_query_ref,
    grad_key_ref,
    grad_value_ref,
):
    length, width = query_ref.shape
    code_width = joined_ref.shape[1]
    grad_code = both_ref[:, :, code_width:].reshape(length, code_width)
    grad_context = times_transposed(grad_code, joined_ref[...]).astype(jnp.bfloat16)
    heads = [slice(start, start + HEAD) for start in range(0, width, HEAD)]
    grads = [grad_context[:, columns] for columns in heads]
    near = [times_transposed(grad, value_ref[:, columns]) for grad, columns in zip(grads, heads)]
    far = [times_transposed(value_ref[:, columns], grad) for grad, columns in zip(grads, heads)]
    for head, columns in enumerate(heads):
        grad_value = times(chance_ref[len(heads) + head].astype(jnp.bfloat16), grads[head])
        grad_value_ref[:, columns] = grad_value.astype(jnp.bfloat16)

    def scores(grad_chances, chances, axis):
        grad_chances = grad_chances.astype(jnp.bfloat16).astype(jnp.float32)
        shift = jnp.sum(grad_chances * chances, axis=axis, keepdims=True)
        return (chances * (grad_chances - shift) * HEAD ** (-0.5)).astype(jnp.bfloat16)

    near = [scores(grad, chance_ref[head], 1) for head, grad in enumerate(near)]
    far = [scores(grad, chance_ref[len(heads) + head], 0) for head, grad in enumerate(far)]
    for head, columns in enumerate(heads):
        grad_query = times(near[head], key_ref[:, columns])
        grad_query_ref[:, columns] = grad_query.astype(jnp.bfloat16)
        grad_key = times(far[head], query_ref[:, columns])
        grad_key_ref[:, columns] = grad_key.astype(jnp.bfloat16)


def prepare_kernel(
    places_ref,
    residual_ref,
    upstream_ref,
    gain_ref,
    bias_ref,
    here_ref,
    gain_here_ref,
    bias_here_ref,
    residual_rows_ref,
    scaled_rows_ref,
):
    length = residual_ref.shape[0]
    rows, width = residual_rows_ref.shape
    part = gain_here_ref.shape[1] // 2
    rank = places_ref[0]
    gain = gain_ref[...]

    def centered(ref, start, scale):
        wide = ref[pl.ds(start, rows), :].astype(jnp.float32)
        wide = wide if scale is None else wide * scale
        return wide - jnp.sum(wide, axis=-1, keepdims=True) / width

    count = width // part // 2

    def places(half):
        start = pl.multiple_of((rank + half * count) * part, HEAD)
        return slice(half * part, (half + 1) * part), pl.ds(start, part)

    for half in range(2):
        here, there = places(half)
        gain_here_ref[:, here] = gain_ref[:, there]
        bias_here_ref[:, here] = bias_ref[:, there]
    for start in range(0, length, rows):
        block = slice(start, start + rows)
        wide = residual_ref[block, :].astype(jnp.float32)
        mean = jnp.sum(wide, axis=-1, keepdims=True) / width
        wide = upstream_ref[block, :].astype(jnp.float32) * gain
        scaled_mean = jnp.sum(wide, axis=-1, keepdims=True) / width
        for half in range(2):
            here, there = places(half)
            scaled = upstream_ref[block, there].astype(jnp.float32) * gain_ref[:, there]
            here_ref[0, block, here] = (scaled - scaled_mean).astype(jnp.bfloat16)
            local = residual_ref[block, there].astype(jnp.float32) - mean
            upper = local.astype(jnp.bfloat16)
            here_ref[1, block, here] = upper
            here_ref[2, block, here] = (local - upper.astype(jnp.float32)).astype(jnp.bfloat16)
    own = pl.multiple_of(rank * rows, rows)
    residual_rows_ref[...] = centered(residual_ref, own, None)
    scaled_rows_ref[...] = centered(upstream_ref, own, gain)


def on_device(
    residual,
    queries,
    key_vectors,
    value_vectors,
    block_mask,
    out_weight,
    codebook,
    norm_gain,
    norm_bias,
    receiver_order,
    upstream,
):
    n_dp = lax.axis_size("dp")
    n_tensor = lax.axis_size("tensor")
    rank = lax.axis_index("tensor")
    length, width = residual.shape[2:]
    code_book = codebook[0]
    shard, code_width = code_book.shape
    piece = shard // n_tensor
    rows = length // n_tensor
    features = n_dp * piece
    heads = queries.shape[3] // HEAD
    share = out_weight.shape[1] // n_dp
    bf16, f32 = jnp.bfloat16, jnp.float32
    dp_rank = lax.axis_index("dp")
    wanted = swapped_2(receiver_order[0], "section", 0)
    places = jnp.stack([rank, dp_rank // N_LOW, dp_rank % N_LOW, wanted[0]])
    slices = [[slice_at(place, t) for place in range(n_dp)] for t in range(n_tensor)]
    slices = lax.dynamic_index_in_dim(jnp.array(slices, jnp.int32), rank, 0, keepdims=False)
    places = jnp.concatenate([places, slices])
    allowed = allowed_pairs(block_mask[0, 0]).astype(f32)

    joined_part = times(out_weight[0], code_book).astype(bf16)
    joined_parts = exchanged(joined_part.reshape(N_LOW, -1, code_width), "dp", LOW_GROUPS)
    own_slice = lax.dynamic_slice_in_dim(code_book, rank * piece, piece, 0)
    own_slice = transposed_owner(own_slice, n_tensor)
    here, gain_here, bias_here, residual_rows, scaled_rows = call(
        prepare_kernel,
        [
            ((3, length, features), bf16),
            ((1, features), f32),
            ((1, features), f32),
            ((rows, width), f32),
            ((rows, width), f32),
        ],
        residual[0, 0],
        upstream[0, 0],
        norm_gain,
        norm_bias,
        places=places,
        after=(joined_part,),
        far_out=(0, 3, 4),
    )
    (joined_rows,) = call(
        first_kernel, [((N_HIGH * share, code_width), bf16)], joined_parts, after=(own_slice, gain_here)
    )
    joined_parts = exchanged(joined_rows.reshape(N_HIGH, share, code_width), "dp", HIGH_GROUPS)
    context, chances = call(
        attend_kernel,
        [((length, heads * HEAD), bf16), ((2 * heads, length, length), f32)],
        queries[0, 0],
        key_vectors[0, 0],
        value_vectors[0, 0],
        allowed,
        after=(joined_rows,),
    )
    (joined_rows,) = call(
        second_kernel, [((N_HIGH, share, code_width), bf16)], joined_parts, after=(context,)
    )
    joined_rows = exchanged(joined_rows, "dp", HIGH_GROUPS)
    sent, own_slice = call(
        third_kernel,
        [((N_LOW, N_HIGH * share, code_width), bf16), ((piece, code_width), bf16)],
        joined_rows.reshape(N_HIGH * share, code_width),
        own_slice,
    )
    joined = exchanged(sent, "dp", LOW_GROUPS).reshape(n_dp * share, code_width)

    (column,) = call(
        stack_kernel,
        [((N_HIGH, piece, code_width), bf16)],
        own_slice,
        *[turned(own_slice, step, 0) for step in range(1, N_HIGH)],
        places=places,
    )
    sent, column = call(
        code_kernel,
        [((n_tensor, length, code_width), bf16), ((N_HIGH, piece, code_width), bf16)],
        context,
        joined,
        column,
        far_out=(0, 1),
    )
    columns = [column] + [turned(column, 0, step) for step in range(1, N_LOW)]
    code_parts = exchanged(sent, "tensor")
    (pack,) = call(
        pack_kernel,
        [((features + 3 * length + EXTRA_ROWS, code_width), bf16)],
        *columns,
        here,
        gain_here,
        bias_here,
        places=places,
        far=(0, N_LOW),
        far_out=(0,),
    )
    (sent,) = call(
        feature_kernel,
        [((n_tensor, rows, 3 * code_width + features + code_width // 2), bf16)],
        code_parts,
        pack,
        gain_here,
        far=(1,),
        raw=(1,),
        scratch=[pltpu.VMEM(pack.shape, bf16), pltpu.SemaphoreType.DMA((2,))],
    )
    arrived = exchanged(sent, "tensor")
    codes, grad_code, grad_residual, orders = call(
        row_kernel,
        [
            ((n_dp, rows, code_width), bf16),
            ((rows, code_width), bf16),
            ((rows, width), bf16),
            ((n_tensor, EXTRA_ROWS, HEAD), f32),
        ],
        arrived,
        residual_rows,
        scaled_rows,
    )

    blocks = exchanged(codes, "dp")
    (both,) = call(
        slot_kernel,
        [((n_tensor, rows, 2 * code_width), bf16)],
        orders,
        blocks,
        grad_code,
    )
    both = exchanged(both, "tensor")
    (chosen,) = call(chosen_kernel, [((rows, code_width), bf16)], both, places=wanted)
    received = swapped_2(chosen, "section", 0)
    grad_query, grad_key, grad_value = call(
        back_kernel,
        [((length, heads * HEAD), bf16)] * 3,
        both,
        joined,
        queries[0, 0],
        key_vectors[0, 0],
        value_vectors[0, 0],
        chances,
        after=(chosen,),
    )
    return (
        received[None, None],
        grad_residual[None, None],
        grad_query[None, None],
        grad_key[None, None],
        grad_value[None, None],
    )


def solution(mesh):
    in_specs = (
        P("section", "dp", None, None),
        P("section", "dp", None, "tensor"),
        P("section", "dp", None, "tensor"),
        P("section", "dp", None, "tensor"),
        P("section", "dp", None, None),
        P("section", "tensor", "dp"),
        P("section", "dp", None),
        P("section", None),
        P("section", None),
        P("section", ("dp", "tensor")),
        P("section", "dp", None, None),
    )
    out_specs = (
        P("section", ("dp", "tensor"), None, None),
        P("section", "dp", "tensor", None),
        P("section", "dp", None, "tensor"),
        P("section", "dp", None, "tensor"),
        P("section", "dp", None, "tensor"),
    )
    return jax.shard_map(
        on_device, mesh=mesh, in_specs=in_specs, out_specs=out_specs, check_vma=False
    )
```

```python
import jax
import jax.numpy as jnp
from jax import lax
from jax.experimental import pallas as pl
from jax.experimental.pallas import tpu as pltpu
from jax.sharding import PartitionSpec as P

HEAD = 128
L = 128
BLK = 32


EPSILON = 1e-05
N_HIGH = 4
N_LOW = 4
N_TENSOR = 8
EXTRA_ROWS = 16
ORDER_ROW = 12
VMEM_BYTES = 12 * 1024 * 1024
HIGH_GROUPS = [[z * N_LOW + y for z in range(N_HIGH)] for y in range(N_LOW)]
LOW_GROUPS = [[z * N_LOW + y for y in range(N_LOW)] for z in range(N_HIGH)]


def swapped_2(value, axis, distance):
    return lax.ppermute(value, axis, [(i, i ^ 1 << distance) for i in range(lax.axis_size(axis))])


def exchanged(value, axis, groups=None):
    return lax.all_to_all(value, axis, 0, 0, axis_index_groups=groups)


def turned(value, high, low):
    pairs = [
        (z * N_LOW + y, (z + high) % N_HIGH * N_LOW + (y + low) % N_LOW)
        for z in range(N_HIGH)
        for y in range(N_LOW)
    ]
    return lax.ppermute(value, "dp", pairs)


def slice_at(place, rank):
    count = N_TENSOR
    owner = place // count * count + rank
    near = [(ring(owner // N_LOW, e // N_LOW) * 2 + ring(owner, e), e) for e in octet_of(place)]
    far = [(-ring(p // 2, rank // 2) - abs(p % 2 - rank % 2), p) for p in range(count)]
    pairs = {e: p for (_, e), (_, p) in zip(sorted(near), sorted(far))}
    return pairs[place]


def octet_of(place):
    start = place // N_TENSOR * N_TENSOR
    return range(start, start + N_TENSOR)


def ring(one, other):
    away = (one - other) % N_LOW
    return min(away, N_LOW - away)


def transposed_owner(value, count):
    pairs = []
    for place in range(2 * count):
        for rank in range(count):
            owner = place // count * count + rank
            pairs.append((owner * count + slice_at(place, rank), place * count + rank))
    return lax.ppermute(value, ("dp", "tensor"), pairs)


def summed(pieces):
    return jnp.sum(pieces.astype(jnp.float32), axis=0).astype(jnp.bfloat16)


def copies_of(value, count):
    return jnp.broadcast_to(value[None], (count,) + value.shape)


def allowed_pairs(mask_blocks):
    block_table = jnp.repeat(jnp.repeat(mask_blocks, BLK, axis=0), BLK, axis=1) == 1
    position = lax.broadcasted_iota(jnp.int32, (L, L), 0)
    column = lax.broadcasted_iota(jnp.int32, (L, L), 1)
    return block_table & (position >= column)


def times(left_side, right_side):
    return jnp.dot(left_side, right_side, preferred_element_type=jnp.float32)


def times_transposed(left_side, right_side):
    return lax.dot_general(
        left_side, right_side, (((1,), (1,)), ((), ())), preferred_element_type=jnp.float32
    )


def transposed_times(left_side, right_side):
    return lax.dot_general(
        left_side, right_side, (((0,), (0,)), ((), ())), preferred_element_type=jnp.float32
    )


def call(
    kernel, shapes, *inputs, places=None, after=(), far=(), far_out=(), raw=(), scratch=()
):
    skipped = len(after)

    def body(*refs):
        kernel(*refs[skipped:])

    scalars = [] if places is None else [places]
    inputs = [
        pltpu.with_memory_space_constraint(array, pltpu.HBM) if place in far else array
        for place, array in enumerate(inputs)
    ]
    return pl.pallas_call(
        body,
        out_shape=[
            pltpu.HBM(shape, dtype) if place in far_out else jax.ShapeDtypeStruct(shape, dtype)
            for place, (shape, dtype) in enumerate(shapes)
        ],
        in_specs=[pl.BlockSpec(memory_space=pl.ANY)] * skipped
        + [pl.BlockSpec(memory_space=pltpu.SMEM)] * len(scalars)
        + [
            pl.BlockSpec(memory_space=pl.ANY if place in raw else pltpu.VMEM)
            for place in range(len(inputs))
        ],
        out_specs=[
            pl.BlockSpec(memory_space=pl.ANY if raw and place in far_out else pltpu.VMEM)
            for place in range(len(shapes))
        ],
        scratch_shapes=list(scratch),
        cost_estimate=pl.CostEstimate(flops=1, bytes_accessed=4_000_000, transcendentals=0),
        compiler_params=pltpu.CompilerParams(vmem_limit_bytes=VMEM_BYTES),
    )(*after, *scalars, *inputs)


def attend_kernel(query_ref, key_ref, value_ref, allowed_ref, context_ref, chance_ref):
    allowed = allowed_ref[...] > 0.5
    for head in range(query_ref.shape[1] // HEAD):
        columns = slice(head * HEAD, (head + 1) * HEAD)
        scores = times_transposed(query_ref[:, columns], key_ref[:, columns]) * HEAD ** (-0.5)
        scores = jnp.where(allowed, scores, -1e30)
        raised = jnp.exp(scores - jnp.max(scores, axis=-1, keepdims=True))
        chances = raised / jnp.sum(raised, axis=-1, keepdims=True)
        chance_ref[head] = chances
        chance_ref[chance_ref.shape[0] // 2 + head] = chances.T
        mixture = times(chances.astype(jnp.bfloat16), value_ref[:, columns])
        context_ref[:, columns] = mixture.astype(jnp.bfloat16)


def first_kernel(parts_ref, out_ref):
    total = parts_ref[0].astype(jnp.float32)
    for part in range(1, parts_ref.shape[0]):
        total += parts_ref[part].astype(jnp.float32)
    out_ref[...] = total.astype(jnp.bfloat16)


def second_kernel(parts_ref, out_ref):
    total = parts_ref[0].astype(jnp.float32)
    for part in range(1, parts_ref.shape[0]):
        total += parts_ref[part].astype(jnp.float32)
    total = total.astype(jnp.bfloat16)
    for copy in range(out_ref.shape[0]):
        out_ref[copy] = total


def third_kernel(parts_ref, slice_ref, out_ref, slice_copy_ref):
    slice_copy_ref[...] = slice_ref[...]
    for copy in range(out_ref.shape[0]):
        out_ref[copy] = parts_ref[...]


def stack_kernel(places_ref, *refs):
    for step in range(N_HIGH):
        refs[-1][(places_ref[1] + N_HIGH - step) % N_HIGH] = refs[step][...]


def code_kernel(context_ref, joined_ref, column_ref, code_ref, column_copy_ref):
    column_copy_ref[...] = column_ref[...]
    code = times(context_ref[...], joined_ref[...]).astype(jnp.bfloat16)
    for copy in range(code_ref.shape[0]):
        code_ref[copy] = code


def total_kernel(parts_ref, out_ref):
    total = parts_ref[0].astype(jnp.float32)
    for part in range(1, parts_ref.shape[0]):
        total += parts_ref[part].astype(jnp.float32)
    total = total.astype(jnp.bfloat16)
    for copy in range(out_ref.shape[0]):
        out_ref[copy] = total


def feature_kernel(places_ref, parts_ref, *refs):
    columns_hbm, (here_hbm, gain_ref, bias_ref, out_ref) = refs[:N_LOW], refs[N_LOW : N_LOW + 4]
    columns_ref, here_ref, book_ref, semaphores = refs[N_LOW + 4 :]
    count, rows, _ = out_ref.shape
    features, width = book_ref.shape
    copies = [
        pltpu.make_async_copy(column, columns_ref.at[step], semaphores.at[step])
        for step, column in enumerate(columns_hbm)
    ]
    copies.append(pltpu.make_async_copy(here_hbm, here_ref, semaphores.at[N_LOW]))
    for copy in copies:
        copy.start()
    total = parts_ref[0].astype(jnp.float32)
    for part in range(1, count):
        total += parts_ref[part].astype(jnp.float32)
    code = total.astype(jnp.bfloat16)
    for step in range(N_LOW):
        copies[step].wait()
        for high in range(N_HIGH):
            piece = columns_ref[step, high]
            place = high * N_LOW + (places_ref[2] + N_LOW - step) % N_LOW
            part = place // N_TENSOR * N_TENSOR + places_ref[4 + place]
            start = pl.multiple_of(part * piece.shape[0], EXTRA_ROWS)
            book_ref[pl.ds(start, piece.shape[0])] = piece
    book = book_ref[...]

    def put(start, value):
        value = value.astype(jnp.bfloat16)
        out_ref[:, :, start : start + value.shape[1]] = value.reshape(count, rows, -1)

    decoded = times_transposed(code, book)
    put(3 * width, decoded)
    copies[N_LOW].wait()
    put(2 * width, times(here_ref[0], book))
    hidden = here_ref[1].astype(jnp.float32) + here_ref[2].astype(jnp.float32) + decoded
    put(0, times(hidden.astype(jnp.bfloat16), book))
    put(width, times((hidden * gain_ref[...]).astype(jnp.bfloat16), book))
    row = lax.broadcasted_iota(jnp.int32, (EXTRA_ROWS, features), 0)
    rest = jnp.where(row == 0, 1.0, jnp.where(row == 1, gain_ref[...], 0.0))
    rest = jnp.where(row == 2, bias_ref[...], rest)
    sums = jnp.zeros((EXTRA_ROWS, width), jnp.float32)
    for _ in range(3):
        top = rest.astype(jnp.bfloat16)
        rest = rest - top.astype(jnp.float32)
        sums += times(top, book)
    upper = sums.astype(jnp.bfloat16).astype(jnp.float32)
    lower = pltpu.roll(sums - upper, 3, 0)
    row = lax.broadcasted_iota(jnp.int32, sums.shape, 0)
    both = jnp.where(row < 3, upper, jnp.where(row < 6, lower, 0.0))
    half = width // 2
    extra = both[:, :half] + pltpu.roll(both[:, half:], 6, 0)
    wanted = places_ref[3].astype(jnp.float32)
    extra = jnp.where(row[:, :half] == ORDER_ROW, wanted, extra).astype(jnp.bfloat16)
    for copy in range(count):
        out_ref[copy, :, 3 * width + features :] = extra


def row_kernel(
    arrived_ref, residual_ref, scaled_ref, codes_ref, grad_code_ref, grad_ref, order_ref
):
    count = arrived_ref.shape[0]
    size = residual_ref.shape[1]
    width = codes_ref.shape[2]
    part = size // count // 2
    last = 3 * width + 2 * part
    total = arrived_ref[0, :, : 3 * width].astype(jnp.float32)
    extra = arrived_ref[0, :, last:].astype(jnp.float32)
    order_ref[0] = extra[:, :HEAD]
    for rank in range(1, count):
        total += arrived_ref[rank, :, : 3 * width].astype(jnp.float32)
        part_extra = arrived_ref[rank, :, last:].astype(jnp.float32)
        order_ref[rank] = part_extra[:, :HEAD]
        extra += part_extra
    sums = extra + pltpu.roll(extra, EXTRA_ROWS - 3, 0)
    sums = jnp.concatenate([sums, pltpu.roll(sums, EXTRA_ROWS - 6, 0)], axis=1)
    ones_sum, gain_sum, bias_sum = sums[0:1], sums[1:2], sums[2:3]
    hidden_code = total[:, :width]
    gained_code = total[:, width : 2 * width]
    scaled_code = total[:, 2 * width :]
    decoded = [
        arrived_ref[rank, :, 3 * width + half * part : 3 * width + (half + 1) * part]
        for half in range(2)
        for rank in range(count)
    ]
    hidden = residual_ref[...] + jnp.concatenate(decoded, axis=1).astype(jnp.float32)
    mean = jnp.sum(hidden, axis=-1, keepdims=True) / size
    centered = hidden - mean
    variance = jnp.sum(centered * centered, axis=-1, keepdims=True) / size
    inv_std = lax.rsqrt(variance + EPSILON)
    scaled = scaled_ref[...]
    product = jnp.sum(scaled * centered, axis=-1, keepdims=True) / size
    share = inv_std * inv_std * product
    grad_ref[...] = (inv_std * (scaled - centered * share)).astype(jnp.bfloat16)
    codes = inv_std * (gained_code - mean * gain_sum) + bias_sum
    grad_code = inv_std * (scaled_code - share * (hidden_code - mean * ones_sum))
    grad_code_ref[...] = grad_code.astype(jnp.bfloat16)
    codes = codes.astype(jnp.bfloat16)
    for copy in range(codes_ref.shape[0]):
        codes_ref[copy] = codes


def slot_kernel(order_ref, blocks_ref, grad_code_ref, out_ref):
    width = grad_code_ref.shape[1]
    for slot in range(out_ref.shape[0]):
        wanted = jnp.max(order_ref[slot, ORDER_ROW : ORDER_ROW + 1]).astype(jnp.int32)
        out_ref[slot, :, :width] = blocks_ref[wanted // N_TENSOR]
        out_ref[slot, :, width:] = grad_code_ref[...]


def chosen_kernel(wanted_ref, both_ref, out_ref):
    out_ref[...] = both_ref[wanted_ref[0] % N_TENSOR, :, : out_ref.shape[1]]


def back_kernel(
    both_ref,
    joined_ref,
    query_ref,
    key_ref,
    value_ref,
    chance_ref,
    grad_query_ref,
    grad_key_ref,
    grad_value_ref,
):
    length, width = query_ref.shape
    code_width = joined_ref.shape[1]
    grad_code = both_ref[:, :, code_width:].reshape(length, code_width)
    grad_context = times_transposed(grad_code, joined_ref[...]).astype(jnp.bfloat16)
    heads = [slice(start, start + HEAD) for start in range(0, width, HEAD)]
    grads = [grad_context[:, columns] for columns in heads]
    near = [times_transposed(grad, value_ref[:, columns]) for grad, columns in zip(grads, heads)]
    far = [times_transposed(value_ref[:, columns], grad) for grad, columns in zip(grads, heads)]
    for head, columns in enumerate(heads):
        grad_value = times(chance_ref[len(heads) + head].astype(jnp.bfloat16), grads[head])
        grad_value_ref[:, columns] = grad_value.astype(jnp.bfloat16)

    def scores(grad_chances, chances, axis):
        grad_chances = grad_chances.astype(jnp.bfloat16).astype(jnp.float32)
        shift = jnp.sum(grad_chances * chances, axis=axis, keepdims=True)
        return (chances * (grad_chances - shift) * HEAD ** (-0.5)).astype(jnp.bfloat16)

    near = [scores(grad, chance_ref[head], 1) for head, grad in enumerate(near)]
    far = [scores(grad, chance_ref[len(heads) + head], 0) for head, grad in enumerate(far)]
    for head, columns in enumerate(heads):
        grad_query = times(near[head], key_ref[:, columns])
        grad_query_ref[:, columns] = grad_query.astype(jnp.bfloat16)
        grad_key = times(far[head], query_ref[:, columns])
        grad_key_ref[:, columns] = grad_key.astype(jnp.bfloat16)


def prepare_kernel(
    places_ref,
    residual_ref,
    upstream_ref,
    gain_ref,
    bias_ref,
    here_ref,
    gain_here_ref,
    bias_here_ref,
    residual_rows_ref,
    scaled_rows_ref,
):
    length = residual_ref.shape[0]
    rows, width = residual_rows_ref.shape
    part = gain_here_ref.shape[1] // 2
    rank = places_ref[0]
    gain = gain_ref[...]

    def centered(ref, start, scale):
        wide = ref[pl.ds(start, rows), :].astype(jnp.float32)
        wide = wide if scale is None else wide * scale
        return wide - jnp.sum(wide, axis=-1, keepdims=True) / width

    count = width // part // 2

    def places(half):
        start = pl.multiple_of((rank + half * count) * part, HEAD)
        return slice(half * part, (half + 1) * part), pl.ds(start, part)

    for half in range(2):
        here, there = places(half)
        gain_here_ref[:, here] = gain_ref[:, there]
        bias_here_ref[:, here] = bias_ref[:, there]
    for start in range(0, length, rows):
        block = slice(start, start + rows)
        wide = residual_ref[block, :].astype(jnp.float32)
        mean = jnp.sum(wide, axis=-1, keepdims=True) / width
        wide = upstream_ref[block, :].astype(jnp.float32) * gain
        scaled_mean = jnp.sum(wide, axis=-1, keepdims=True) / width
        for half in range(2):
            here, there = places(half)
            scaled = upstream_ref[block, there].astype(jnp.float32) * gain_ref[:, there]
            here_ref[0, block, here] = (scaled - scaled_mean).astype(jnp.bfloat16)
            local = residual_ref[block, there].astype(jnp.float32) - mean
            upper = local.astype(jnp.bfloat16)
            here_ref[1, block, here] = upper
            here_ref[2, block, here] = (local - upper.astype(jnp.float32)).astype(jnp.bfloat16)
    own = pl.multiple_of(rank * rows, rows)
    residual_rows_ref[...] = centered(residual_ref, own, None)
    scaled_rows_ref[...] = centered(upstream_ref, own, gain)


def on_device(
    residual,
    queries,
    key_vectors,
    value_vectors,
    block_mask,
    out_weight,
    codebook,
    norm_gain,
    norm_bias,
    receiver_order,
    upstream,
):
    n_dp = lax.axis_size("dp")
    n_tensor = lax.axis_size("tensor")
    rank = lax.axis_index("tensor")
    length, width = residual.shape[2:]
    code_book = codebook[0]
    shard, code_width = code_book.shape
    piece = shard // n_tensor
    rows = length // n_tensor
    features = n_dp * piece
    heads = queries.shape[3] // HEAD
    share = out_weight.shape[1] // n_dp
    bf16, f32 = jnp.bfloat16, jnp.float32
    dp_rank = lax.axis_index("dp")
    wanted = swapped_2(receiver_order[0], "section", 0)
    places = jnp.stack([rank, dp_rank // N_LOW, dp_rank % N_LOW, wanted[0]])
    slices = [[slice_at(place, t) for place in range(n_dp)] for t in range(n_tensor)]
    slices = lax.dynamic_index_in_dim(jnp.array(slices, jnp.int32), rank, 0, keepdims=False)
    places = jnp.concatenate([places, slices])
    allowed = allowed_pairs(block_mask[0, 0]).astype(f32)

    joined_part = times(out_weight[0], code_book).astype(bf16)
    joined_parts = exchanged(joined_part.reshape(N_LOW, -1, code_width), "dp", LOW_GROUPS)
    own_slice = lax.dynamic_slice_in_dim(code_book, rank * piece, piece, 0)
    own_slice = transposed_owner(own_slice, n_tensor)
    here, gain_here, bias_here, residual_rows, scaled_rows = call(
        prepare_kernel,
        [
            ((3, length, features), bf16),
            ((1, features), f32),
            ((1, features), f32),
            ((rows, width), f32),
            ((rows, width), f32),
        ],
        residual[0, 0],
        upstream[0, 0],
        norm_gain,
        norm_bias,
        places=places,
        after=(joined_part,),
        far_out=(0, 3, 4),
    )
    (joined_rows,) = call(
        first_kernel, [((N_HIGH * share, code_width), bf16)], joined_parts, after=(own_slice, gain_here)
    )
    joined_parts = exchanged(joined_rows.reshape(N_HIGH, share, code_width), "dp", HIGH_GROUPS)
    context, chances = call(
        attend_kernel,
        [((length, heads * HEAD), bf16), ((2 * heads, length, length), f32)],
        queries[0, 0],
        key_vectors[0, 0],
        value_vectors[0, 0],
        allowed,
        after=(joined_rows,),
    )
    (joined_rows,) = call(
        second_kernel, [((N_HIGH, share, code_width), bf16)], joined_parts, after=(context,)
    )
    joined_rows = exchanged(joined_rows, "dp", HIGH_GROUPS)
    sent, own_slice = call(
        third_kernel,
        [((N_LOW, N_HIGH * share, code_width), bf16), ((piece, code_width), bf16)],
        joined_rows.reshape(N_HIGH * share, code_width),
        own_slice,
    )
    joined = exchanged(sent, "dp", LOW_GROUPS).reshape(n_dp * share, code_width)

    (column,) = call(
        stack_kernel,
        [((N_HIGH, piece, code_width), bf16)],
        own_slice,
        *[turned(own_slice, step, 0) for step in range(1, N_HIGH)],
        places=places,
    )
    sent, column = call(
        code_kernel,
        [((n_tensor, length, code_width), bf16), ((N_HIGH, piece, code_width), bf16)],
        context,
        joined,
        column,
        far_out=(0, 1),
    )
    columns = [column] + [turned(column, 0, step) for step in range(1, N_LOW)]
    code_parts = exchanged(sent, "tensor")
    (sent,) = call(
        feature_kernel,
        [((n_tensor, rows, 3 * code_width + features + code_width // 2), bf16)],
        code_parts,
        *columns,
        here,
        gain_here,
        bias_here,
        places=places,
        far=range(1, N_LOW + 2),
        raw=range(1, N_LOW + 2),
        scratch=[
            pltpu.VMEM((N_LOW,) + column.shape, bf16),
            pltpu.VMEM(here.shape, bf16),
            pltpu.VMEM((features, code_width), bf16),
            pltpu.SemaphoreType.DMA((N_LOW + 1,)),
        ],
    )
    arrived = exchanged(sent, "tensor")
    codes, grad_code, grad_residual, orders = call(
        row_kernel,
        [
            ((n_dp, rows, code_width), bf16),
            ((rows, code_width), bf16),
            ((rows, width), bf16),
            ((n_tensor, EXTRA_ROWS, HEAD), f32),
        ],
        arrived,
        residual_rows,
        scaled_rows,
    )

    blocks = exchanged(codes, "dp")
    (both,) = call(
        slot_kernel,
        [((n_tensor, rows, 2 * code_width), bf16)],
        orders,
        blocks,
        grad_code,
    )
    both = exchanged(both, "tensor")
    (chosen,) = call(chosen_kernel, [((rows, code_width), bf16)], both, places=wanted)
    received = swapped_2(chosen, "section", 0)
    grad_query, grad_key, grad_value = call(
        back_kernel,
        [((length, heads * HEAD), bf16)] * 3,
        both,
        joined,
        queries[0, 0],
        key_vectors[0, 0],
        value_vectors[0, 0],
        chances,
        after=(chosen,),
    )
    return (
        received[None, None],
        grad_residual[None, None],
        grad_query[None, None],
        grad_key[None, None],
        grad_value[None, None],
    )


def solution(mesh):
    in_specs = (
        P("section", "dp", None, None),
        P("section", "dp", None, "tensor"),
        P("section", "dp", None, "tensor"),
        P("section", "dp", None, "tensor"),
        P("section", "dp", None, None),
        P("section", "tensor", "dp"),
        P("section", "dp", None),
        P("section", None),
        P("section", None),
        P("section", ("dp", "tensor")),
        P("section", "dp", None, None),
    )
    out_specs = (
        P("section", ("dp", "tensor"), None, None),
        P("section", "dp", "tensor", None),
        P("section", "dp", None, "tensor"),
        P("section", "dp", None, "tensor"),
        P("section", "dp", None, "tensor"),
    )
    return jax.shard_map(
        on_device, mesh=mesh, in_specs=in_specs, out_specs=out_specs, check_vma=False
    )
```

```python
import jax
import jax.numpy as jnp
from jax import lax
from jax.experimental import pallas as pl
from jax.experimental.pallas import tpu as pltpu
from jax.sharding import PartitionSpec as P

HEAD = 128
L = 128
BLK = 32


EPSILON = 1e-05
N_HIGH = 4
N_LOW = 4
N_TENSOR = 8
EXTRA_ROWS = 16
ORDER_ROW = 12
VMEM_BYTES = 12 * 1024 * 1024
HIGH_GROUPS = [[z * N_LOW + y for z in range(N_HIGH)] for y in range(N_LOW)]
LOW_GROUPS = [[z * N_LOW + y for y in range(N_LOW)] for z in range(N_HIGH)]


def swapped_2(value, axis, distance):
    return lax.ppermute(value, axis, [(i, i ^ 1 << distance) for i in range(lax.axis_size(axis))])


def exchanged(value, axis, groups=None):
    return lax.all_to_all(value, axis, 0, 0, axis_index_groups=groups)


def turned(value, high, low):
    pairs = [
        (z * N_LOW + y, (z + high) % N_HIGH * N_LOW + (y + low) % N_LOW)
        for z in range(N_HIGH)
        for y in range(N_LOW)
    ]
    return lax.ppermute(value, "dp", pairs)


def slice_at(place, rank):
    count = N_TENSOR
    owner = place // count * count + rank
    near = [(ring(owner // N_LOW, e // N_LOW) * 2 + ring(owner, e), e) for e in octet_of(place)]
    far = [(-ring(p // 2, rank // 2) - abs(p % 2 - rank % 2), p) for p in range(count)]
    pairs = {e: p for (_, e), (_, p) in zip(sorted(near), sorted(far))}
    return pairs[place]


def octet_of(place):
    start = place // N_TENSOR * N_TENSOR
    return range(start, start + N_TENSOR)


def ring(one, other):
    away = (one - other) % N_LOW
    return min(away, N_LOW - away)


def transposed_owner(value, count):
    pairs = []
    for place in range(2 * count):
        for rank in range(count):
            owner = place // count * count + rank
            pairs.append((owner * count + slice_at(place, rank), place * count + rank))
    return lax.ppermute(value, ("dp", "tensor"), pairs)


def summed(pieces):
    return jnp.sum(pieces.astype(jnp.float32), axis=0).astype(jnp.bfloat16)


def copies_of(value, count):
    return jnp.broadcast_to(value[None], (count,) + value.shape)


def allowed_pairs(mask_blocks):
    block_table = jnp.repeat(jnp.repeat(mask_blocks, BLK, axis=0), BLK, axis=1) == 1
    position = lax.broadcasted_iota(jnp.int32, (L, L), 0)
    column = lax.broadcasted_iota(jnp.int32, (L, L), 1)
    return block_table & (position >= column)


def times(left_side, right_side):
    return jnp.dot(left_side, right_side, preferred_element_type=jnp.float32)


def times_transposed(left_side, right_side):
    return lax.dot_general(
        left_side, right_side, (((1,), (1,)), ((), ())), preferred_element_type=jnp.float32
    )


def transposed_times(left_side, right_side):
    return lax.dot_general(
        left_side, right_side, (((0,), (0,)), ((), ())), preferred_element_type=jnp.float32
    )


def call(
    kernel, shapes, *inputs, places=None, after=(), far=(), far_out=(), raw=(), scratch=()
):
    skipped = len(after)

    def body(*refs):
        kernel(*refs[skipped:])

    scalars = [] if places is None else [places]
    inputs = [
        pltpu.with_memory_space_constraint(array, pltpu.HBM) if place in far else array
        for place, array in enumerate(inputs)
    ]
    return pl.pallas_call(
        body,
        out_shape=[
            pltpu.HBM(shape, dtype) if place in far_out else jax.ShapeDtypeStruct(shape, dtype)
            for place, (shape, dtype) in enumerate(shapes)
        ],
        in_specs=[pl.BlockSpec(memory_space=pl.ANY)] * skipped
        + [pl.BlockSpec(memory_space=pltpu.SMEM)] * len(scalars)
        + [
            pl.BlockSpec(memory_space=pl.ANY if place in raw else pltpu.VMEM)
            for place in range(len(inputs))
        ],
        out_specs=[
            pl.BlockSpec(memory_space=pl.ANY if raw and place in far_out else pltpu.VMEM)
            for place in range(len(shapes))
        ],
        scratch_shapes=list(scratch),
        cost_estimate=pl.CostEstimate(flops=1, bytes_accessed=4_000_000, transcendentals=0),
        compiler_params=pltpu.CompilerParams(vmem_limit_bytes=VMEM_BYTES),
    )(*after, *scalars, *inputs)


def attend_kernel(query_ref, key_ref, value_ref, allowed_ref, context_ref, chance_ref):
    allowed = allowed_ref[...] > 0.5
    for head in range(query_ref.shape[1] // HEAD):
        columns = slice(head * HEAD, (head + 1) * HEAD)
        scores = times_transposed(query_ref[:, columns], key_ref[:, columns]) * HEAD ** (-0.5)
        scores = jnp.where(allowed, scores, -1e30)
        raised = jnp.exp(scores - jnp.max(scores, axis=-1, keepdims=True))
        chances = raised / jnp.sum(raised, axis=-1, keepdims=True)
        chance_ref[head] = chances
        chance_ref[chance_ref.shape[0] // 2 + head] = chances.T
        mixture = times(chances.astype(jnp.bfloat16), value_ref[:, columns])
        context_ref[:, columns] = mixture.astype(jnp.bfloat16)


def first_kernel(parts_ref, out_ref):
    total = parts_ref[0].astype(jnp.float32)
    for part in range(1, parts_ref.shape[0]):
        total += parts_ref[part].astype(jnp.float32)
    out_ref[...] = total.astype(jnp.bfloat16)


def second_kernel(parts_ref, out_ref):
    total = parts_ref[0].astype(jnp.float32)
    for part in range(1, parts_ref.shape[0]):
        total += parts_ref[part].astype(jnp.float32)
    total = total.astype(jnp.bfloat16)
    for copy in range(out_ref.shape[0]):
        out_ref[copy] = total


def third_kernel(parts_ref, slice_ref, out_ref, slice_copy_ref):
    slice_copy_ref[...] = slice_ref[...]
    for copy in range(out_ref.shape[0]):
        out_ref[copy] = parts_ref[...]


def stack_kernel(places_ref, *refs):
    for step in range(N_HIGH):
        refs[-1][(places_ref[1] + N_HIGH - step) % N_HIGH] = refs[step][...]


def code_kernel(context_ref, joined_ref, column_ref, code_ref, column_copy_ref):
    column_copy_ref[...] = column_ref[...]
    code = times(context_ref[...], joined_ref[...]).astype(jnp.bfloat16)
    for copy in range(code_ref.shape[0]):
        code_ref[copy] = code


def total_kernel(parts_ref, out_ref):
    total = parts_ref[0].astype(jnp.float32)
    for part in range(1, parts_ref.shape[0]):
        total += parts_ref[part].astype(jnp.float32)
    total = total.astype(jnp.bfloat16)
    for copy in range(out_ref.shape[0]):
        out_ref[copy] = total


def feature_kernel(places_ref, parts_ref, *refs):
    columns_hbm, (here_hbm, gain_ref, bias_ref, out_ref) = refs[:N_LOW], refs[N_LOW : N_LOW + 4]
    columns_ref, here_ref, book_ref, semaphores = refs[N_LOW + 4 :]
    count, rows, _ = out_ref.shape
    features, width = book_ref.shape
    copies = [
        pltpu.make_async_copy(column, columns_ref.at[step], semaphores.at[step])
        for step, column in enumerate(columns_hbm)
    ]
    copies.append(pltpu.make_async_copy(here_hbm, here_ref, semaphores.at[N_LOW]))
    for copy in copies:
        copy.start()
    total = parts_ref[0].astype(jnp.float32)
    for part in range(1, count):
        total += parts_ref[part].astype(jnp.float32)
    code = total.astype(jnp.bfloat16)
    for step in range(N_LOW):
        copies[step].wait()
        for high in range(N_HIGH):
            piece = columns_ref[step, high]
            place = high * N_LOW + (places_ref[2] + N_LOW - step) % N_LOW
            part = place // N_TENSOR * N_TENSOR + places_ref[4 + place]
            start = pl.multiple_of(part * piece.shape[0], EXTRA_ROWS)
            book_ref[pl.ds(start, piece.shape[0])] = piece
    book = book_ref[...]

    def put(start, value):
        value = value.astype(jnp.bfloat16)
        out_ref[:, :, start : start + value.shape[1]] = value.reshape(count, rows, -1)

    decoded = times_transposed(code, book)
    put(3 * width, decoded)
    copies[N_LOW].wait()
    hidden = here_ref[1].astype(jnp.float32) + here_ref[2].astype(jnp.float32) + decoded
    row = lax.broadcasted_iota(jnp.int32, (EXTRA_ROWS, features), 0)
    rest = jnp.where(row == 0, 1.0, jnp.where(row == 1, gain_ref[...], 0.0))
    rest = jnp.where(row == 2, bias_ref[...], rest)
    left = [hidden.astype(jnp.bfloat16), (hidden * gain_ref[...]).astype(jnp.bfloat16), here_ref[0]]
    for _ in range(3):
        top = rest.astype(jnp.bfloat16)
        rest = rest - top.astype(jnp.float32)
        left.append(top)
    length = count * rows
    products = times(jnp.concatenate(left, axis=0), book)
    for place in range(3):
        put(place * width, products[place * length : (place + 1) * length])
    sums = products[3 * length : 3 * length + EXTRA_ROWS]
    for place in (1, 2):
        start = 3 * length + place * EXTRA_ROWS
        sums += products[start : start + EXTRA_ROWS]
    upper = sums.astype(jnp.bfloat16).astype(jnp.float32)
    lower = pltpu.roll(sums - upper, 3, 0)
    row = lax.broadcasted_iota(jnp.int32, sums.shape, 0)
    both = jnp.where(row < 3, upper, jnp.where(row < 6, lower, 0.0))
    half = width // 2
    extra = both[:, :half] + pltpu.roll(both[:, half:], 6, 0)
    wanted = places_ref[3].astype(jnp.float32)
    extra = jnp.where(row[:, :half] == ORDER_ROW, wanted, extra).astype(jnp.bfloat16)
    for copy in range(count):
        out_ref[copy, :, 3 * width + features :] = extra


def row_kernel(
    arrived_ref, residual_ref, scaled_ref, codes_ref, grad_code_ref, grad_ref, order_ref
):
    count = arrived_ref.shape[0]
    size = residual_ref.shape[1]
    width = codes_ref.shape[2]
    part = size // count // 2
    last = 3 * width + 2 * part
    total = arrived_ref[0, :, : 3 * width].astype(jnp.float32)
    extra = arrived_ref[0, :, last:].astype(jnp.float32)
    order_ref[0] = extra[:, :HEAD]
    for rank in range(1, count):
        total += arrived_ref[rank, :, : 3 * width].astype(jnp.float32)
        part_extra = arrived_ref[rank, :, last:].astype(jnp.float32)
        order_ref[rank] = part_extra[:, :HEAD]
        extra += part_extra
    sums = extra + pltpu.roll(extra, EXTRA_ROWS - 3, 0)
    sums = jnp.concatenate([sums, pltpu.roll(sums, EXTRA_ROWS - 6, 0)], axis=1)
    ones_sum, gain_sum, bias_sum = sums[0:1], sums[1:2], sums[2:3]
    hidden_code = total[:, :width]
    gained_code = total[:, width : 2 * width]
    scaled_code = total[:, 2 * width :]
    decoded = [
        arrived_ref[rank, :, 3 * width + half * part : 3 * width + (half + 1) * part]
        for half in range(2)
        for rank in range(count)
    ]
    hidden = residual_ref[...] + jnp.concatenate(decoded, axis=1).astype(jnp.float32)
    mean = jnp.sum(hidden, axis=-1, keepdims=True) / size
    centered = hidden - mean
    variance = jnp.sum(centered * centered, axis=-1, keepdims=True) / size
    inv_std = lax.rsqrt(variance + EPSILON)
    scaled = scaled_ref[...]
    product = jnp.sum(scaled * centered, axis=-1, keepdims=True) / size
    share = inv_std * inv_std * product
    grad_ref[...] = (inv_std * (scaled - centered * share)).astype(jnp.bfloat16)
    codes = inv_std * (gained_code - mean * gain_sum) + bias_sum
    grad_code = inv_std * (scaled_code - share * (hidden_code - mean * ones_sum))
    grad_code_ref[...] = grad_code.astype(jnp.bfloat16)
    codes = codes.astype(jnp.bfloat16)
    for copy in range(codes_ref.shape[0]):
        codes_ref[copy] = codes


def slot_kernel(order_ref, blocks_ref, grad_code_ref, out_ref):
    width = grad_code_ref.shape[1]
    for slot in range(out_ref.shape[0]):
        wanted = jnp.max(order_ref[slot, ORDER_ROW : ORDER_ROW + 1]).astype(jnp.int32)
        out_ref[slot, :, :width] = blocks_ref[wanted // N_TENSOR]
        out_ref[slot, :, width:] = grad_code_ref[...]


def chosen_kernel(wanted_ref, both_ref, out_ref):
    out_ref[...] = both_ref[wanted_ref[0] % N_TENSOR, :, : out_ref.shape[1]]


def back_kernel(
    both_ref,
    joined_ref,
    query_ref,
    key_ref,
    value_ref,
    chance_ref,
    grad_query_ref,
    grad_key_ref,
    grad_value_ref,
):
    length, width = query_ref.shape
    code_width = joined_ref.shape[1]
    grad_code = both_ref[:, :, code_width:].reshape(length, code_width)
    grad_context = times_transposed(grad_code, joined_ref[...]).astype(jnp.bfloat16)
    heads = [slice(start, start + HEAD) for start in range(0, width, HEAD)]
    grads = [grad_context[:, columns] for columns in heads]
    near = [times_transposed(grad, value_ref[:, columns]) for grad, columns in zip(grads, heads)]
    far = [times_transposed(value_ref[:, columns], grad) for grad, columns in zip(grads, heads)]
    for head, columns in enumerate(heads):
        grad_value = times(chance_ref[len(heads) + head].astype(jnp.bfloat16), grads[head])
        grad_value_ref[:, columns] = grad_value.astype(jnp.bfloat16)

    def scores(grad_chances, chances, axis):
        grad_chances = grad_chances.astype(jnp.bfloat16).astype(jnp.float32)
        shift = jnp.sum(grad_chances * chances, axis=axis, keepdims=True)
        return (chances * (grad_chances - shift) * HEAD ** (-0.5)).astype(jnp.bfloat16)

    near = [scores(grad, chance_ref[head], 1) for head, grad in enumerate(near)]
    far = [scores(grad, chance_ref[len(heads) + head], 0) for head, grad in enumerate(far)]
    for head, columns in enumerate(heads):
        grad_query = times(near[head], key_ref[:, columns])
        grad_query_ref[:, columns] = grad_query.astype(jnp.bfloat16)
        grad_key = times(far[head], query_ref[:, columns])
        grad_key_ref[:, columns] = grad_key.astype(jnp.bfloat16)


def prepare_kernel(
    places_ref,
    residual_ref,
    upstream_ref,
    gain_ref,
    bias_ref,
    here_ref,
    gain_here_ref,
    bias_here_ref,
    residual_rows_ref,
    scaled_rows_ref,
):
    length = residual_ref.shape[0]
    rows, width = residual_rows_ref.shape
    part = gain_here_ref.shape[1] // 2
    rank = places_ref[0]
    gain = gain_ref[...]

    def centered(ref, start, scale):
        wide = ref[pl.ds(start, rows), :].astype(jnp.float32)
        wide = wide if scale is None else wide * scale
        return wide - jnp.sum(wide, axis=-1, keepdims=True) / width

    count = width // part // 2

    def places(half):
        start = pl.multiple_of((rank + half * count) * part, HEAD)
        return slice(half * part, (half + 1) * part), pl.ds(start, part)

    for half in range(2):
        here, there = places(half)
        gain_here_ref[:, here] = gain_ref[:, there]
        bias_here_ref[:, here] = bias_ref[:, there]
    for start in range(0, length, rows):
        block = slice(start, start + rows)
        wide = residual_ref[block, :].astype(jnp.float32)
        mean = jnp.sum(wide, axis=-1, keepdims=True) / width
        wide = upstream_ref[block, :].astype(jnp.float32) * gain
        scaled_mean = jnp.sum(wide, axis=-1, keepdims=True) / width
        for half in range(2):
            here, there = places(half)
            scaled = upstream_ref[block, there].astype(jnp.float32) * gain_ref[:, there]
            here_ref[0, block, here] = (scaled - scaled_mean).astype(jnp.bfloat16)
            local = residual_ref[block, there].astype(jnp.float32) - mean
            upper = local.astype(jnp.bfloat16)
            here_ref[1, block, here] = upper
            here_ref[2, block, here] = (local - upper.astype(jnp.float32)).astype(jnp.bfloat16)
    own = pl.multiple_of(rank * rows, rows)
    residual_rows_ref[...] = centered(residual_ref, own, None)
    scaled_rows_ref[...] = centered(upstream_ref, own, gain)


def on_device(
    residual,
    queries,
    key_vectors,
    value_vectors,
    block_mask,
    out_weight,
    codebook,
    norm_gain,
    norm_bias,
    receiver_order,
    upstream,
):
    n_dp = lax.axis_size("dp")
    n_tensor = lax.axis_size("tensor")
    rank = lax.axis_index("tensor")
    length, width = residual.shape[2:]
    code_book = codebook[0]
    shard, code_width = code_book.shape
    piece = shard // n_tensor
    rows = length // n_tensor
    features = n_dp * piece
    heads = queries.shape[3] // HEAD
    share = out_weight.shape[1] // n_dp
    bf16, f32 = jnp.bfloat16, jnp.float32
    dp_rank = lax.axis_index("dp")
    wanted = swapped_2(receiver_order[0], "section", 0)
    places = jnp.stack([rank, dp_rank // N_LOW, dp_rank % N_LOW, wanted[0]])
    slices = [[slice_at(place, t) for place in range(n_dp)] for t in range(n_tensor)]
    slices = lax.dynamic_index_in_dim(jnp.array(slices, jnp.int32), rank, 0, keepdims=False)
    places = jnp.concatenate([places, slices])
    allowed = allowed_pairs(block_mask[0, 0]).astype(f32)

    joined_part = times(out_weight[0], code_book).astype(bf16)
    joined_parts = exchanged(joined_part.reshape(N_LOW, -1, code_width), "dp", LOW_GROUPS)
    own_slice = lax.dynamic_slice_in_dim(code_book, rank * piece, piece, 0)
    own_slice = transposed_owner(own_slice, n_tensor)
    here, gain_here, bias_here, residual_rows, scaled_rows = call(
        prepare_kernel,
        [
            ((3, length, features), bf16),
            ((1, features), f32),
            ((1, features), f32),
            ((rows, width), f32),
            ((rows, width), f32),
        ],
        residual[0, 0],
        upstream[0, 0],
        norm_gain,
        norm_bias,
        places=places,
        after=(joined_part,),
        far_out=(0, 3, 4),
    )
    (joined_rows,) = call(
        first_kernel, [((N_HIGH * share, code_width), bf16)], joined_parts, after=(own_slice, gain_here)
    )
    joined_parts = exchanged(joined_rows.reshape(N_HIGH, share, code_width), "dp", HIGH_GROUPS)
    context, chances = call(
        attend_kernel,
        [((length, heads * HEAD), bf16), ((2 * heads, length, length), f32)],
        queries[0, 0],
        key_vectors[0, 0],
        value_vectors[0, 0],
        allowed,
        after=(joined_rows,),
    )
    (joined_rows,) = call(
        second_kernel, [((N_HIGH, share, code_width), bf16)], joined_parts, after=(context,)
    )
    joined_rows = exchanged(joined_rows, "dp", HIGH_GROUPS)
    sent, own_slice = call(
        third_kernel,
        [((N_LOW, N_HIGH * share, code_width), bf16), ((piece, code_width), bf16)],
        joined_rows.reshape(N_HIGH * share, code_width),
        own_slice,
    )
    joined = exchanged(sent, "dp", LOW_GROUPS).reshape(n_dp * share, code_width)

    (column,) = call(
        stack_kernel,
        [((N_HIGH, piece, code_width), bf16)],
        own_slice,
        *[turned(own_slice, step, 0) for step in range(1, N_HIGH)],
        places=places,
    )
    sent, column = call(
        code_kernel,
        [((n_tensor, length, code_width), bf16), ((N_HIGH, piece, code_width), bf16)],
        context,
        joined,
        column,
        far_out=(0, 1),
    )
    columns = [column] + [turned(column, 0, step) for step in range(1, N_LOW)]
    code_parts = exchanged(sent, "tensor")
    (sent,) = call(
        feature_kernel,
        [((n_tensor, rows, 3 * code_width + features + code_width // 2), bf16)],
        code_parts,
        *columns,
        here,
        gain_here,
        bias_here,
        places=places,
        far=range(1, N_LOW + 2),
        raw=range(1, N_LOW + 2),
        scratch=[
            pltpu.VMEM((N_LOW,) + column.shape, bf16),
            pltpu.VMEM(here.shape, bf16),
            pltpu.VMEM((features, code_width), bf16),
            pltpu.SemaphoreType.DMA((N_LOW + 1,)),
        ],
    )
    arrived = exchanged(sent, "tensor")
    codes, grad_code, grad_residual, orders = call(
        row_kernel,
        [
            ((n_dp, rows, code_width), bf16),
            ((rows, code_width), bf16),
            ((rows, width), bf16),
            ((n_tensor, EXTRA_ROWS, HEAD), f32),
        ],
        arrived,
        residual_rows,
        scaled_rows,
    )

    blocks = exchanged(codes, "dp")
    (both,) = call(
        slot_kernel,
        [((n_tensor, rows, 2 * code_width), bf16)],
        orders,
        blocks,
        grad_code,
    )
    both = exchanged(both, "tensor")
    (chosen,) = call(chosen_kernel, [((rows, code_width), bf16)], both, places=wanted)
    received = swapped_2(chosen, "section", 0)
    grad_query, grad_key, grad_value = call(
        back_kernel,
        [((length, heads * HEAD), bf16)] * 3,
        both,
        joined,
        queries[0, 0],
        key_vectors[0, 0],
        value_vectors[0, 0],
        chances,
        after=(chosen,),
    )
    return (
        received[None, None],
        grad_residual[None, None],
        grad_query[None, None],
        grad_key[None, None],
        grad_value[None, None],
    )


def solution(mesh):
    in_specs = (
        P("section", "dp", None, None),
        P("section", "dp", None, "tensor"),
        P("section", "dp", None, "tensor"),
        P("section", "dp", None, "tensor"),
        P("section", "dp", None, None),
        P("section", "tensor", "dp"),
        P("section", "dp", None),
        P("section", None),
        P("section", None),
        P("section", ("dp", "tensor")),
        P("section", "dp", None, None),
    )
    out_specs = (
        P("section", ("dp", "tensor"), None, None),
        P("section", "dp", "tensor", None),
        P("section", "dp", None, "tensor"),
        P("section", "dp", None, "tensor"),
        P("section", "dp", None, "tensor"),
    )
    return jax.shard_map(
        on_device, mesh=mesh, in_specs=in_specs, out_specs=out_specs, check_vma=False
    )
```
